128 devices in a mesh: section: 4 (over x), brick: 32 (over y, z, core).
Axes of the slice: x: 4, y: 4, z: 4, core: 2. Of those that a mesh axis runs over, the one named last changes fastest.
Arguments:
- saved_inputs: bfloat16 [4, 2, 64, 8, 8, 8, 128], P('section', None, 'brick'), may hold values from -6 to 6
- saved_preacts: bfloat16 [4, 2, 64, 8, 8, 8, 128], P('section', None, 'brick'), may hold values from -6 to 6
- supervision: bfloat16 [4, 2, 64, 8, 8, 8, 128], P('section', None, 'brick'), may hold values from -6 to 6
- weights: bfloat16 [4, 3456, 128], P('section'), may hold values from -0.109375 to 0.109375
- trainer: int32 [2, 64], replicated, may hold values from 0 to 31, as said below
- counts: int32 [2, 64], P(None, 'brick'), may hold values from 1 to 512
Outputs:
- skip_grads: bfloat16 [4, 2, 128, 8, 8, 8, 128], P('section', None, 'brick')
- weight_grads: float32 [4, 3456, 128], P('section')
The draws below stay inside these ranges and needn't reach their ends.
Inputs may be any that keep to these rules, and one draw needn't show every extreme that they name: For each micro-batch, an owner's 2 bricks go to 2 different trainers among the owner itself and the 3 owners after it (owner + 0 to owner + 3, modulo 64 // 2); so no trainer receives more than 4 bricks of one micro-batch, and some trainer receives exactly 4.
All inputs are finite; a program needn't handle non-finite values.
Results may differ from the reference program's by a relative error of at most 0.02.
Values may be sent and summed in bfloat16 or wider, within the bound.
No kernel may reach another device: no remote copies, remote signals or barrier semaphores. Data moves between devices by JAX's collectives and lax.ppermute only.
A program may use at most 128 MiB of HBM per device.

```python
import math
import jax
import jax.numpy as jnp
from jax import lax

C = 128
BR = 8
OWN = 2
MICRO = 2
LAYERS = 4
BRICKS = 64
RECV = 4
SLOTS = 128
VOXELS = 512


def draw_trainer(key, part):
    key = jax.random.fold_in(key, 11)
    peer_count = BRICKS // OWN
    owners = jnp.arange(peer_count, dtype=jnp.int32)
    lists = []
    for micro_pos in range(MICRO):
        subkey = jax.random.fold_in(key, micro_pos)
        key_hot, key_score = jax.random.split(subkey)
        hot = jax.random.randint(key_hot, (), 0, peer_count).astype(jnp.int32)
        hot_offset = jnp.mod(hot - owners, peer_count).astype(jnp.int32)
        scores = jax.random.randint(key_score, (peer_count, RECV), 0, 1 << 20).astype(jnp.int32) * RECV + jnp.arange(RECV, dtype=jnp.int32)[None, :]
        forced = hot_offset[:, None] == jnp.arange(RECV, dtype=jnp.int32)[None, :]
        scores = jnp.where(forced, -1, scores)
        chosen = jnp.argsort(scores, axis=1, stable=True)[:, :OWN].astype(jnp.int32)
        targets = jnp.mod(owners[:, None] + chosen, peer_count).astype(jnp.int32)
        lists.append(targets.reshape(BRICKS))
    return jnp.stack(lists)


def with_ends(array, key, low, high):
    place = [jax.random.randint(jax.random.fold_in(key, axis), (), 0, length) for axis, length in enumerate(array.shape)]
    widest = array.shape.index(max(array.shape))
    next_to = place[:widest] + [(place[widest] + 1) % array.shape[widest]] + place[widest + 1:]
    return array.at[tuple(place)].set(low).at[tuple(next_to)].set(high)


def shard_levels(rng, extent, pieces, low, top_value):
    level = 1.0
    for axis_at, parts in pieces:
        steps = jax.random.uniform(jax.random.fold_in(jax.random.fold_in(rng, 6), axis_at), (parts,), jnp.float32, low / len(pieces), top_value / len(pieces))
        level = level * jnp.repeat(jnp.exp(steps), extent[axis_at] // parts).reshape((-1,) + (1,) * (len(extent) - 1 - axis_at))
    return level


def noise(key, shape, scale, bound, pieces=(), kind=jnp.bfloat16):
    values = jax.random.normal(key, shape, jnp.float32) * scale
    if len(pieces) > 0:
        values = shard_levels(key, shape, pieces, -0.22, 0.18) * values
    return jnp.clip(values, min=-bound, max=bound).astype(kind)


def setup_inputs(seed: int = 0) -> dict:
    streams_of = jax.random.split(jax.random.key(seed), 7)
    return {
        "saved_inputs": noise(streams_of[0], (LAYERS, MICRO, BRICKS, BR, BR, BR, C), 1.0, 6.0, ((0, 4), (2, 32))),
        "saved_preacts": noise(streams_of[1], (LAYERS, MICRO, BRICKS, BR, BR, BR, C), 1.0, 6.0, ((0, 4), (2, 32))),
        "supervision": noise(streams_of[2], (LAYERS, MICRO, BRICKS, BR, BR, BR, C), 1.0, 6.0, ((0, 4), (2, 32))),
        "weights": noise(streams_of[3], (LAYERS, 27 * C, C), (27 * C) ** -0.5, 0.109375, ((0, 4),)),
        "trainer": draw_trainer(jax.random.fold_in(streams_of[6], 71), 0),
        "counts": with_ends(jax.random.randint(streams_of[5], (MICRO, BRICKS), 1, VOXELS + 1), jax.random.fold_in(streams_of[5], 1), 1, VOXELS).astype(jnp.int32),
    }


def columns(brick):
    brick_edge = brick.shape[0]
    padded = jnp.pad(brick, ((1, 1), (1, 1), (1, 1), (0, 0)))
    shifted = [padded[a:a + brick_edge, b:b + brick_edge, c:c + brick_edge, :] for a in range(3) for b in range(3) for c in range(3)]
    return jnp.concatenate(shifted, axis=-1).reshape(brick_edge * brick_edge * brick_edge, -1)

def silu_slope(preacts):
    sigmoid_pre = jax.nn.sigmoid(preacts)
    return sigmoid_pre * (1.0 + preacts * (1.0 - sigmoid_pre))

def brick_backward(weight_full, inputs_one, preacts_one, grad_out):
    deltas = (grad_out * silu_slope(preacts_one.astype(jnp.float32))).astype(jnp.bfloat16)
    flat_deltas = deltas.astype(jnp.float32).reshape(-1, weight_full.shape[1])
    inputs_full = inputs_one.astype(jnp.float32)
    col_inputs = columns(inputs_full)
    weight_part = jnp.dot(col_inputs.T, flat_deltas, precision=lax.Precision.HIGHEST)
    col_grads = jnp.dot(flat_deltas, weight_full.T, precision=lax.Precision.HIGHEST)
    primal_out, pull_back = jax.vjp(columns, inputs_full)
    grad_input = pull_back(col_grads)[0]
    return (grad_input.astype(jnp.bfloat16), weight_part)

def reference(saved_inputs, saved_preacts, supervision, weights, trainer, counts):
    label_share = counts.astype(jnp.float32) / VOXELS
    weighted = (supervision.astype(jnp.float32) * label_share[None, :, :, None, None, None, None]).astype(jnp.bfloat16)
    peer_count = BRICKS // OWN
    owner_of = jnp.arange(BRICKS, dtype=jnp.int32) // OWN
    positions = []
    for micro_pos in range(MICRO):
        targets = trainer[micro_pos].astype(jnp.int32)
        distance = jnp.mod(targets - owner_of, peer_count).astype(jnp.int32)
        positions.append((targets * RECV + distance).astype(jnp.int32))
    sums_by_layer = [jnp.zeros((27 * C, C), jnp.float32) for layer_pos in range(LAYERS)]
    grads_by_layer = [[None] * MICRO for layer_pos in range(LAYERS)]
    for micro_pos in range(MICRO):
        above = jnp.zeros(saved_inputs.shape[2:], jnp.bfloat16)
        for layer_pos in range(LAYERS - 1, -1, -1):
            weight_full = weights[layer_pos].astype(jnp.float32)
            grad_out = above.astype(jnp.float32) + weighted[layer_pos, micro_pos].astype(jnp.float32)

            def visit(running, element):
                grad_input, weight_part = brick_backward(weight_full, element[0], element[1], element[2])
                return (running + weight_part, grad_input)
            new_sum, grad_inputs = lax.scan(visit, sums_by_layer[layer_pos], (saved_inputs[layer_pos, micro_pos], saved_preacts[layer_pos, micro_pos], grad_out))
            sums_by_layer[layer_pos] = new_sum
            empty_slots = jnp.zeros((SLOTS,) + saved_inputs.shape[3:], jnp.bfloat16)
            grads_by_layer[layer_pos][micro_pos] = empty_slots.at[positions[micro_pos]].set(grad_inputs)
            above = grad_inputs
    skip_grads = jnp.stack([jnp.stack(grads_by_layer[layer_pos]) for layer_pos in range(LAYERS)])
    norm_factor = 1.0 / math.sqrt(MICRO * BRICKS * VOXELS)
    weight_grads = jnp.stack(sums_by_layer) * norm_factor
    return (skip_grads, weight_grads)
```

```python
import functools
import math

import jax
import jax.numpy as jnp
from jax import lax
from jax.experimental import pallas as pl
from jax.experimental.pallas import tpu as pltpu
from jax.sharding import PartitionSpec as P

C = 128
VOX = 512
ANY = pl.BlockSpec(memory_space=pl.ANY)
F32 = jnp.float32
BF16 = jnp.bfloat16


def shift_rows(block, by):
    if by == 0:
        return block
    pad = jnp.zeros((abs(by),) + block.shape[1:], block.dtype)
    if by > 0:
        return jnp.concatenate([pad, block[:-by]], axis=0)
    return jnp.concatenate([block[-by:], pad], axis=0)


def tick_kernel(tick, info, share, p_ref, sup_ref, above_ref, w_ref, *rest):
    gin_ref, pd_all, pd, sem = rest[-4:]

    @pl.when(info[tick, 1] == 1)
    def _():
        scale = share[info[tick, 0]]
        p = p_ref[0].astype(F32)
        weighted = (sup_ref[0].astype(F32) * scale).astype(BF16).astype(F32)
        grad = weighted + above_ref[...].astype(F32)
        sig = jax.nn.sigmoid(p)
        delta = (grad * (sig * (1.0 + p * (1.0 - sig)))).reshape(64, 8, C)
        place = lax.broadcasted_iota(jnp.int32, (64, 8, C), 1)
        for w in (-1, 0, 1):
            if w == 0:
                moved = delta
            elif w == 1:
                moved = jnp.where(place == 0, 0.0, pltpu.roll(delta, 1, 1))
            else:
                moved = jnp.where(place == 7, 0.0, pltpu.roll(delta, 7, 1))
            moved = moved.reshape(8, 8, 8, C)
            zero = jnp.zeros((8, 1, 8, C), F32)
            for v in (-1, 0, 1):
                if v == 0:
                    out = moved
                elif v == 1:
                    out = jnp.concatenate([zero, moved[:, :-1]], axis=1)
                else:
                    out = jnp.concatenate([moved[:, 1:], zero], axis=1)
                at = ((v + 1) * 3 + (w + 1)) * C
                pd[:, at : at + C] = out.reshape(VOX, C).astype(BF16)
        copy = pltpu.make_async_copy(pd, pd_all.at[tick], sem)
        copy.start()
        y = jnp.dot(pd[...], w_ref[...], preferred_element_type=F32)
        gin = y[:, C : 2 * C] + shift_rows(y[:, :C], -64) + shift_rows(y[:, 2 * C :], 64)
        gin_ref[...] = gin.astype(BF16)
        copy.wait()


def tick_step(tick, ticks, info, share, preacts, sup, above, w_all, pd_all):
    one = lambda i, info, share: (info[tick, 0], 0, 0)
    flat = lambda i, info, share: (0, 0)
    in_specs = [
        pl.BlockSpec((1, VOX, C), one),
        pl.BlockSpec((1, VOX, C), one),
        pl.BlockSpec((VOX, C), flat),
        pl.BlockSpec((9 * C, 3 * C), flat),
    ]
    operands = [preacts, sup, above, w_all]
    aliases = {}
    if pd_all is not None:
        in_specs.append(ANY)
        operands.append(pd_all)
        aliases = {6: 1}
    return pl.pallas_call(
        functools.partial(tick_kernel, tick),
        grid_spec=pltpu.PrefetchScalarGridSpec(
            num_scalar_prefetch=2,
            grid=(1,),
            in_specs=in_specs,
            out_specs=[pl.BlockSpec((VOX, C), flat), ANY],
            scratch_shapes=[pltpu.VMEM((VOX, 9 * C), BF16), pltpu.SemaphoreType.DMA],
        ),
        out_shape=[
            jax.ShapeDtypeStruct((VOX, C), BF16),
            jax.ShapeDtypeStruct((ticks, VOX, 9 * C), BF16),
        ],
        input_output_aliases=aliases,
        compiler_params=pltpu.CompilerParams(vmem_limit_bytes=24 << 20),
        cost_estimate=pl.CostEstimate(
            flops=2 * VOX * 27 * C * C, bytes_accessed=4 << 20, transcendentals=VOX * C
        ),
        name="tick%d" % tick,
    )(info, share, *operands)


def weight_kernel(place, pd_ref, x_ref, keep_ref, send_ref, acc):
    step = pl.program_id(0)
    x = x_ref[0]
    x3 = jnp.concatenate([shift_rows(x, 64), x, shift_rows(x, -64)], axis=1)
    part = lax.dot_general(
        x3, pd_ref[0], (((0,), (0,)), ((), ())), preferred_element_type=F32
    )

    @pl.when(step == 0)
    def _():
        acc[...] = part

    @pl.when(step > 0)
    def _():
        acc[...] += part

    @pl.when(step == 3)
    def _():
        mine = pl.multiple_of(place[1] * 192, 16)
        other = pl.multiple_of(192 - place[1] * 192, 16)
        keep_ref[...] = acc[pl.ds(mine, 192), :].astype(BF16)
        send_ref[...] = acc[pl.ds(other, 192), :].astype(BF16)


def weight_step(place, pd_all, inputs):
    half = jax.ShapeDtypeStruct((192, 9 * C), BF16)
    flat = lambda i, place: (0, 0)
    return pl.pallas_call(
        weight_kernel,
        grid_spec=pltpu.PrefetchScalarGridSpec(
            num_scalar_prefetch=1,
            grid=(4,),
            in_specs=[
                pl.BlockSpec((1, VOX, 9 * C), lambda i, place: (i + place[0], 0, 0)),
                pl.BlockSpec((1, VOX, C), lambda i, place: (i, 0, 0)),
            ],
            out_specs=[pl.BlockSpec((192, 9 * C), flat)] * 2,
            scratch_shapes=[pltpu.VMEM((384, 9 * C), F32)],
        ),
        out_shape=[half, half],
        compiler_params=pltpu.CompilerParams(vmem_limit_bytes=32 << 20),
        cost_estimate=pl.CostEstimate(
            flops=8 * VOX * 27 * C * C, bytes_accessed=7 << 20, transcendentals=0
        ),
        name="weight_terms",
    )(place, pd_all, inputs)


def pack_kernel(ticks, pick, *rest):
    gins = rest[:ticks]
    outs = rest[ticks : ticks + 4]
    zero, sems = rest[ticks + 4 :]
    zero[...] = jnp.zeros_like(zero)
    for d in range(4):
        for m in range(2):
            for t in range(-1, ticks):

                @pl.when(pick[m, d] == t)
                def _(t=t, d=d, m=m):
                    src = zero if t < 0 else gins[t]
                    pltpu.make_async_copy(src, outs[d].at[m], sems.at[d, m]).start()

    for d in range(4):
        for m in range(2):
            pltpu.make_async_copy(zero, outs[d].at[m], sems.at[d, m]).wait()


def pack_step(pick, gins):
    return pl.pallas_call(
        functools.partial(pack_kernel, len(gins)),
        grid_spec=pltpu.PrefetchScalarGridSpec(
            num_scalar_prefetch=1,
            grid=(1,),
            in_specs=[ANY] * len(gins),
            out_specs=[ANY] * 4,
            scratch_shapes=[pltpu.VMEM((VOX, C), BF16), pltpu.SemaphoreType.DMA((4, 2))],
        ),
        out_shape=[jax.ShapeDtypeStruct((2, VOX, C), BF16)] * 4,
        name="pack_slots",
    )(pick, *gins)


def finish_kernel(scale, place, mine_ref, other_ref, out_ref):
    core, z = place[1], place[2]
    for ref, half in ((mine_ref, core), (other_ref, 1 - core)):
        for k in range(4):
            first = half * 12 + lax.bitwise_xor(z, k) * 3
            for i in range(3):
                group = first + i
                u = group // 8
                row = pl.multiple_of(u * (9 * C) + (group - u * 8) * 16, 16)
                rows = ref[k, i * 16 : (i + 1) * 16, :].astype(F32) * scale
                for tap in range(9):
                    out_ref[pl.ds(row + tap * C, 16), :] = rows[:, tap * C : (tap + 1) * C]


def finish_step(scale, place, mine, other):
    whole = lambda i, place: (0, 0, 0)
    return pl.pallas_call(
        functools.partial(finish_kernel, scale),
        grid_spec=pltpu.PrefetchScalarGridSpec(
            num_scalar_prefetch=1,
            grid=(1,),
            in_specs=[pl.BlockSpec((4, 48, 9 * C), whole)] * 2,
            out_specs=pl.BlockSpec((27 * C, C), lambda i, place: (0, 0)),
        ),
        out_shape=jax.ShapeDtypeStruct((27 * C, C), F32),
        compiler_params=pltpu.CompilerParams(vmem_limit_bytes=24 << 20),
        name="finish_weights",
    )(place, mine, other)


def swap(block, bit):
    pairs = [(i, i ^ bit) for i in range(lax.axis_size("brick"))]
    return lax.ppermute(block, "brick", pairs)


def shifted(block, distance):
    n = lax.axis_size("brick")
    return lax.ppermute(block, "brick", [(i, (i + distance) % n) for i in range(n)])


def shards(saved_inputs, saved_preacts, supervision, weights, trainer, counts):
    peers = lax.axis_size("brick")
    me = lax.axis_index("brick")
    layers = lax.axis_size("section")
    section = lax.axis_index("section")
    micros, own = saved_inputs.shape[1:3]
    work = micros * own
    ticks = layers + work - 1
    core = jnp.mod(me, 2)
    z = jnp.mod(me // 2, 4)

    inputs = saved_inputs.reshape(work, VOX, C)
    preacts = saved_preacts.reshape(work, VOX, C)
    sup = supervision.reshape(work, VOX, C)
    w_all = (
        weights[0].reshape(3, 9, C, C).transpose(1, 3, 0, 2).reshape(9 * C, 3 * C)
    )
    share = counts.reshape(work).astype(F32) / VOX
    late = layers - 1 - section
    index = jnp.arange(ticks, dtype=jnp.int32) - late
    info = jnp.stack(
        [jnp.clip(index, 0, work - 1), ((index >= 0) & (index < work)).astype(jnp.int32)], axis=1
    )
    place = jnp.stack([late, core, z]).astype(jnp.int32)
    targets = lax.dynamic_slice_in_dim(trainer, me * own, own, 1)
    offsets = jnp.mod(targets - me, peers)
    match = offsets[:, :, None] == jnp.arange(4, dtype=jnp.int32)[None, None, :]
    brick = jnp.arange(work, dtype=jnp.int32).reshape(micros, own)
    pick = jnp.max(jnp.where(match, (brick + late)[:, :, None], -1), axis=1).astype(jnp.int32)

    above = jnp.zeros((VOX, C), BF16)
    pd_all = None
    gins = []
    for tick in range(ticks):
        gin, pd_all = tick_step(tick, ticks, info, share, preacts, sup, above, w_all, pd_all)
        gins.append(gin)
        if tick + 1 < ticks:
            above = lax.ppermute(gin, "section", [(i, i - 1) for i in range(1, layers)])

    keep, send = weight_step(place, pd_all, inputs)
    local, *sent = pack_step(pick, gins)
    slots = [local] + [shifted(block, d + 1) for d, block in enumerate(sent)]
    skip_grads = jnp.stack(slots, axis=1).reshape((1, micros, 4) + saved_inputs.shape[3:])

    half = keep.astype(F32) + swap(send, 1).astype(F32)
    half = half.astype(BF16).reshape(4, 48, 9 * C)
    part = [lax.dynamic_index_in_dim(half, lax.bitwise_xor(z, k), 0, False) for k in range(4)]
    total = part[0].astype(F32)
    for k in (2, 1, 3):
        total = total + swap(part[k], 2 * k).astype(F32)
    total = total.astype(BF16)
    full = total.astype(F32)
    for k in (2, 1, 3):
        full = full + swap(total, 8 * k).astype(F32)
    full = full.astype(BF16)
    mine = jnp.stack([full] + [swap(full, 2 * k) for k in (1, 2, 3)])
    other = swap(mine, 1)
    scale = 1.0 / math.sqrt(work * peers * VOX)
    weight_grads = finish_step(scale, place, mine, other)
    return skip_grads, weight_grads[None]


def solution(mesh):
    bricks = P("section", None, "brick", None, None, None, None)
    in_specs = (bricks, bricks, bricks, P("section", None, None), P(), P(None, "brick"))
    out_specs = (bricks, P("section", None, None))
    return jax.shard_map(shards, mesh=mesh, in_specs=in_specs, out_specs=out_specs, check_vma=False)
```

```python
import functools
import math

import jax
import jax.numpy as jnp
from jax import lax
from jax.experimental import pallas as pl
from jax.experimental.pallas import tpu as pltpu
from jax.sharding import PartitionSpec as P

C = 128
VOX = 512
TAPS = 27
WORK = 4
LAG = 4
F32 = jnp.float32
BF16 = jnp.bfloat16
ANY = pl.BlockSpec(memory_space=pl.ANY)
VM = pl.BlockSpec(memory_space=pltpu.VMEM)
SM = pl.BlockSpec(memory_space=pltpu.SMEM)
Y_BITS = (8, 16, 24)
Z_BITS = (2, 4, 6)


def shape(dims, dtype=BF16):
    return jax.ShapeDtypeStruct(dims, dtype)


def vmem(x):
    return pltpu.with_memory_space_constraint(x, pltpu.MemorySpace.VMEM)


def params():
    return pltpu.CompilerParams(vmem_limit_bytes=16 << 20)


def shift_rows(block, by):
    if by == 0:
        return block
    pad = jnp.zeros((abs(by),) + block.shape[1:], block.dtype)
    if by > 0:
        return jnp.concatenate([pad, block[:-by]], axis=0)
    return jnp.concatenate([block[-by:], pad], axis=0)


def deltas_of(share, p, sup, above):
    p = p.astype(F32)
    weighted = (sup.astype(F32).reshape(64, 8, C) * share[None]).reshape(VOX, C)
    grad = weighted.astype(BF16).astype(F32) + above.astype(F32)
    sig = jax.nn.sigmoid(p)
    return grad * (sig * (1.0 + p * (1.0 - sig)))


def spread(delta, pd):
    delta = delta.reshape(64, 8, C)
    place = lax.broadcasted_iota(jnp.int32, (64, 8, C), 1)
    for w in (-1, 0, 1):
        if w == 0:
            moved = delta
        elif w == 1:
            moved = jnp.where(place == 0, 0.0, pltpu.roll(delta, 1, 1))
        else:
            moved = jnp.where(place == 7, 0.0, pltpu.roll(delta, 7, 1))
        moved = moved.reshape(8, 8, 8, C)
        zero = jnp.zeros((8, 1, 8, C), F32)
        for v in (-1, 0, 1):
            if v == 0:
                out = moved
            elif v == 1:
                out = jnp.concatenate([zero, moved[:, :-1]], axis=1)
            else:
                out = jnp.concatenate([moved[:, 1:], zero], axis=1)
            at = ((v + 1) * 3 + (w + 1)) * C
            pd[:, at : at + C] = out.reshape(VOX, C).astype(BF16)


def input_grad(pd, wn):
    y = lax.dot_general(pd, wn, (((1,), (1,)), ((), ())), preferred_element_type=F32)
    gin = y[:, C : 2 * C] + shift_rows(y[:, :C], -64) + shift_rows(y[:, 2 * C :], 64)
    return gin.astype(BF16)


def position(slot):
    late = lax.axis_size("section") - 1 - lax.axis_index("section")
    index = slot - LAG * late
    return (index >= 0) & (index < WORK), jnp.clip(index, 0, WORK - 1)


def first_kernel(
    c_hbm, p_hbm, sup_hbm, w_hbm, gin_ref, gins, deltas, wn, p_ref, sup_ref, shares, pd, w_ref, counts, sems
):
    active, _ = position(0)
    rest = pl.ds(1, WORK - 1)
    copies = [
        pltpu.make_async_copy(c_hbm, counts, sems.at[5]),
        pltpu.make_async_copy(p_hbm.at[0], p_ref.at[0], sems.at[0]),
        pltpu.make_async_copy(sup_hbm.at[0], sup_ref.at[0], sems.at[1]),
        pltpu.make_async_copy(w_hbm, w_ref, sems.at[2]),
        pltpu.make_async_copy(p_hbm.at[rest], p_ref.at[rest], sems.at[3]),
        pltpu.make_async_copy(sup_hbm.at[rest], sup_ref.at[rest], sems.at[4]),
    ]
    for copy in copies:
        copy.start()
    copies[0].wait()
    for brick in range(WORK):
        count = counts[brick // 2, brick % 2].astype(F32)
        shares[brick] = jnp.full((8, C), count * (1.0 / VOX), F32)
    copies[1].wait()
    copies[2].wait()

    @pl.when(active)
    def _():
        zero = jnp.zeros((VOX, C), BF16)
        delta = deltas_of(shares[0], p_ref[0], sup_ref[0], zero)
        deltas[0] = delta.astype(BF16)
        spread(delta, pd)

    copies[3].wait()
    for u in range(3):
        for tap in range(9):
            at = (u * 9 + tap) * C
            wn[u * C : (u + 1) * C, tap * C : (tap + 1) * C] = w_ref[at : at + C, :]

    @pl.when(active)
    def _():
        gin = input_grad(pd[...], wn[...])
        gin_ref[...] = gin
        gins[0] = gin

    copies[4].wait()
    copies[5].wait()


def first_step(counts, preacts, sup, weights):
    hbm = lambda x: pltpu.with_memory_space_constraint(x, pltpu.MemorySpace.HBM)
    bricks = pltpu.VMEM((WORK, VOX, C), BF16)
    return pl.pallas_call(
        first_kernel,
        in_specs=[ANY] * 4,
        out_specs=[VM] * 7,
        out_shape=[
            shape((VOX, C)),
            bricks,
            bricks,
            pltpu.VMEM((3 * C, 9 * C), BF16),
            bricks,
            bricks,
            pltpu.VMEM((WORK, 8, C), F32),
        ],
        scratch_shapes=[
            pltpu.VMEM((VOX, 9 * C), BF16),
            pltpu.VMEM((TAPS * C, C), BF16),
            pltpu.SMEM((2, 2), jnp.int32),
            pltpu.SemaphoreType.DMA((6,)),
        ],
        compiler_params=params(),
        name="tick_first",
    )(hbm(counts), hbm(preacts), hbm(sup), hbm(weights))


def tick_kernel(slot, sends, shares, p_ref, sup_ref, above_ref, wn, gins_in, deltas_in, *outs):
    gins, deltas, pd = outs[0], outs[1], outs[-1]
    active, brick = position(slot)

    @pl.when(active)
    def _():
        delta = deltas_of(shares[brick], p_ref[brick], sup_ref[brick], above_ref[...])
        deltas[brick] = delta.astype(BF16)
        spread(delta, pd)
        gin = input_grad(pd[...], wn[...])
        gins[brick] = gin
        if sends:
            outs[2][...] = gin


def tick_step(slot, sends, shares, preacts, sup, above, wn, gins, deltas):
    bricks = pltpu.VMEM((WORK, VOX, C), BF16)
    return pl.pallas_call(
        functools.partial(tick_kernel, slot, sends),
        in_specs=[VM] * 7,
        out_specs=[VM] * (2 + sends),
        out_shape=[bricks, bricks] + [shape((VOX, C))] * sends,
        scratch_shapes=[pltpu.VMEM((VOX, 9 * C), BF16)],
        input_output_aliases={5: 0, 6: 1},
        compiler_params=params(),
        cost_estimate=pl.CostEstimate(
            flops=2 * VOX * TAPS * C * C, bytes_accessed=2 << 20, transcendentals=VOX * C
        ),
        name="tick%d" % slot,
    )(vmem(shares), vmem(preacts), vmem(sup), above, vmem(wn), vmem(gins), vmem(deltas))


def transpose_kernel(x_ref, out):
    for brick in range(WORK):
        x = x_ref[brick].T
        pad = jnp.zeros((C, 64), BF16)
        out[brick, :C, :] = jnp.concatenate([pad, x[:, :-64]], axis=1)
        out[brick, C : 2 * C, :] = x
        out[brick, 2 * C :, :] = jnp.concatenate([x[:, 64:], pad], axis=1)


def transpose_step(inputs):
    return pl.pallas_call(
        transpose_kernel,
        in_specs=[VM],
        out_specs=VM,
        out_shape=shape((WORK, 3 * C, VOX)),
        compiler_params=params(),
        name="inputs_across",
    )(inputs)


def early_kernel(deltas, xt, acc, pd):
    spread(deltas[0].astype(F32), pd.at[0])
    total = jnp.dot(xt[0], pd[0], preferred_element_type=F32)
    spread(deltas[1].astype(F32), pd.at[1])
    acc[...] = total + jnp.dot(xt[1], pd[1], preferred_element_type=F32)


def early_step(deltas, xt):
    return pl.pallas_call(
        early_kernel,
        in_specs=[VM] * 2,
        out_specs=VM,
        out_shape=shape((3 * C, 9 * C), F32),
        scratch_shapes=[pltpu.VMEM((2, VOX, 9 * C), BF16)],
        compiler_params=params(),
        cost_estimate=pl.CostEstimate(
            flops=4 * VOX * TAPS * C * C, bytes_accessed=4 << 20, transcendentals=0
        ),
        name="weight_terms_early",
    )(deltas, xt)


def late_kernel(
    slot, shares, p_ref, sup_ref, above_ref, deltas, xt, acc_in, keep_ref, send_ref, pd, pd_2, acc
):
    active, _ = position(slot)
    last = WORK - 1
    spread(deltas[last - 1].astype(F32), pd_2)
    total = acc_in[...] + jnp.dot(xt[last - 1], pd_2[...], preferred_element_type=F32)

    @pl.when(active)
    def _():
        spread(deltas_of(shares[last], p_ref[last], sup_ref[last], above_ref[...]), pd)

    @pl.when(jnp.logical_not(active))
    def _():
        spread(deltas[last].astype(F32), pd)

    acc[...] = total + jnp.dot(xt[last], pd[...], preferred_element_type=F32)
    core = lax.rem(lax.axis_index("brick"), 2)
    mine = pl.multiple_of(core * 192, 16)
    other = pl.multiple_of(192 - core * 192, 16)
    send_ref[...] = acc[pl.ds(other, 192), :].astype(BF16)
    keep_ref[...] = acc[pl.ds(mine, 192), :].astype(BF16)


def late_step(slot, shares, preacts, sup, above, deltas, xt, acc):
    return pl.pallas_call(
        functools.partial(late_kernel, slot),
        in_specs=[VM] * 7,
        out_specs=[VM] * 3,
        out_shape=[shape((192, 9 * C))] * 2 + [shape((VOX, 9 * C))],
        scratch_shapes=[pltpu.VMEM((VOX, 9 * C), BF16), pltpu.VMEM((3 * C, 9 * C), F32)],
        compiler_params=params(),
        cost_estimate=pl.CostEstimate(
            flops=4 * VOX * TAPS * C * C, bytes_accessed=7 << 20, transcendentals=0
        ),
        name="weight_terms",
    )(vmem(shares), vmem(preacts), vmem(sup), above, vmem(deltas), xt, acc)


def pack_kernel(slot, pick, gins, pd, wn, local, *sent):
    active, _ = position(slot)
    zero = jnp.zeros((VOX, C), BF16)
    outs = (local,) + sent

    def put(micro, first, second):
        for d in range(4):
            which = pick[micro, d]
            outs[d][micro] = jnp.where(which == 0, first, jnp.where(which == 1, second, zero))

    put(0, gins[0], gins[1])

    @pl.when(active)
    def _():
        put(1, gins[2], input_grad(pd[...], wn[...]))

    @pl.when(jnp.logical_not(active))
    def _():
        put(1, gins[2], gins[3])


def pack_step(slot, pick, gins, pd, wn):
    return pl.pallas_call(
        functools.partial(pack_kernel, slot),
        in_specs=[SM] + [VM] * 3,
        out_specs=[VM] * 4,
        out_shape=[shape((2, VOX, C))] * 4,
        compiler_params=params(),
        cost_estimate=pl.CostEstimate(
            flops=2 * VOX * TAPS * C * C, bytes_accessed=4 << 20, transcendentals=0
        ),
        name="pack",
    )(pick, vmem(gins), pd, vmem(wn))


def slots_kernel(*refs):
    blocks, out, sems = refs[:4], refs[4], refs[5]
    copies = [
        pltpu.make_async_copy(block.at[micro], out.at[micro, d], sems.at[d, micro])
        for d, block in enumerate(blocks)
        for micro in range(2)
    ]
    for copy in copies:
        copy.start()
    for copy in copies:
        copy.wait()


def slots_step(blocks):
    return pl.pallas_call(
        slots_kernel,
        in_specs=[VM] * 4,
        out_specs=ANY,
        out_shape=shape((2, 4, VOX, C)),
        scratch_shapes=[pltpu.SemaphoreType.DMA((4, 2))],
        compiler_params=params(),
        name="slots",
    )(*blocks)


def finish_kernel(scale, mine, other, out_hbm, out, sems):
    me = lax.axis_index("brick")
    core = lax.rem(me, 2)
    label = lax.div(me, 8)
    copies = []
    for u in range(3):
        for i in range(8):
            group = u * 8 + i
            half, part, row = group // 12, group % 12 // 3, group % 3 * 16
            at = lax.bitwise_xor(label, part)
            rows = jnp.where(core == half, mine[at, row : row + 16], other[at, row : row + 16])
            rows = rows.astype(F32) * scale
            for tap in range(9):
                to = (u * 9 + tap) * C + i * 16
                out[to : to + 16, :] = rows[:, tap * C : (tap + 1) * C]
        size = 9 * C
        copies.append(
            pltpu.make_async_copy(
                out.at[u * size : (u + 1) * size], out_hbm.at[u * size : (u + 1) * size], sems.at[u]
            )
        )
        copies[-1].start()
    for copy in copies:
        copy.wait()


def finish_step(scale, mine, other):
    return pl.pallas_call(
        functools.partial(finish_kernel, scale),
        in_specs=[VM] * 2,
        out_specs=ANY,
        out_shape=shape((TAPS * C, C), F32),
        scratch_shapes=[pltpu.VMEM((TAPS * C, C), F32), pltpu.SemaphoreType.DMA((3,))],
        compiler_params=params(),
        name="finish_weights",
    )(mine, other)


def swap(block, bits):
    pairs = [(i, i ^ bits) for i in range(lax.axis_size("brick"))]
    return lax.ppermute(block, "brick", pairs)


def shifted(block, distance):
    n = lax.axis_size("brick")
    return lax.ppermute(block, "brick", [(i, (i + distance) % n) for i in range(n)])


def shards(saved_inputs, saved_preacts, supervision, weights, trainer, counts):
    peers = lax.axis_size("brick")
    me = lax.axis_index("brick")
    layers = lax.axis_size("section")
    micros, own = saved_inputs.shape[1:3]
    slots = WORK + LAG * (layers - 1)

    inputs = saved_inputs.reshape(WORK, VOX, C)
    preacts = saved_preacts.reshape(WORK, VOX, C)
    sup = supervision.reshape(WORK, VOX, C)
    targets = lax.dynamic_slice_in_dim(trainer, me * own, own, 1)
    offsets = jnp.mod(targets - me, peers)
    match = offsets[:, :, None] == jnp.arange(4, dtype=jnp.int32)[None, None, :]
    brick = jnp.arange(own, dtype=jnp.int32)
    pick = jnp.max(jnp.where(match, brick[None, :, None], -1), axis=1).astype(jnp.int32)

    above = {}
    gin, gins, deltas, wn, preacts, sup, shares = first_step(counts, preacts, sup, weights[0])
    zero = jnp.zeros((VOX, C), BF16)
    xt = transpose_step(inputs)
    for slot in range(slots - 1):
        senders = [s for s in range(1, layers) if 0 <= slot - LAG * (layers - 1 - s) < WORK]
        if slot > 0:
            gins, deltas, *sent = tick_step(
                slot, len(senders) > 0, shares, preacts, sup, above.get(slot, zero), wn, gins, deltas
            )
            gin = sent[0] if sent else None
        if senders:
            above[slot + LAG] = lax.ppermute(gin, "section", [(s, s - 1) for s in senders])
        if slot == slots - 3:
            acc = early_step(deltas, xt)
    last = slots - 1
    keep, send, pd = late_step(last, shares, preacts, sup, above[last], deltas, xt, acc)
    from_core = swap(send, 1)
    local, send_1, send_2, send_3 = pack_step(last, pick, gins, pd, wn)
    from_3 = shifted(send_3, 3)
    from_core, send_1, send_2 = lax.optimization_barrier((from_core, send_1, send_2))

    half = (keep.astype(F32) + from_core.astype(F32)).astype(BF16).reshape(4, 48, 9 * C)
    y = me // 8
    part = [lax.dynamic_index_in_dim(half, lax.bitwise_xor(y, k), 0, False) for k in range(4)]
    total = part[0].astype(F32)
    for k, bits in enumerate(Y_BITS):
        total = total + swap(part[k + 1], bits).astype(F32)
    total, from_3 = lax.optimization_barrier((total.astype(BF16), from_3))
    full = total.astype(F32)
    for bits in Z_BITS:
        full = full + swap(total, bits).astype(F32)
    full, send_1, send_2 = lax.optimization_barrier((full.astype(BF16), send_1, send_2))
    got = [swap(full, bits) for bits in Y_BITS] + [shifted(send_1, 1), shifted(send_2, 2)]
    *got, from_1, from_2 = lax.optimization_barrier(got)
    blocks = [local, from_1, from_2, from_3]
    skip_grads = slots_step(blocks).reshape((1, micros, 4) + saved_inputs.shape[3:])
    mine = jnp.stack([full] + got)
    other = swap(mine, 1)
    scale = 1.0 / math.sqrt(WORK * peers * VOX)
    weight_grads = finish_step(scale, mine, other)
    return skip_grads, weight_grads[None]


def solution(mesh):
    bricks = P("section", None, "brick", None, None, None, None)
    in_specs = (bricks, bricks, bricks, P("section", None, None), P(), P(None, "brick"))
    out_specs = (bricks, P("section", None, None))
    return jax.shard_map(shards, mesh=mesh, in_specs=in_specs, out_specs=out_specs, check_vma=False)
```

```python
import functools
import math

import jax
import jax.numpy as jnp
from jax import lax
from jax.experimental import pallas as pl
from jax.experimental.pallas import tpu as pltpu
from jax.sharding import PartitionSpec as P

C = 128
VOX = 512
TAPS = 27
WORK = 4
F32 = jnp.float32
BF16 = jnp.bfloat16
ANY = pl.BlockSpec(memory_space=pl.ANY)
VM = pl.BlockSpec(memory_space=pltpu.VMEM)
SM = pl.BlockSpec(memory_space=pltpu.SMEM)
Y_BITS = (8, 16, 24)
Z_BITS = (2, 4, 6)


def shape(dims, dtype=BF16):
    return jax.ShapeDtypeStruct(dims, dtype)


def vmem(x):
    return pltpu.with_memory_space_constraint(x, pltpu.MemorySpace.VMEM)


def params():
    return pltpu.CompilerParams(vmem_limit_bytes=16 << 20)


def shift_rows(block, by):
    if by == 0:
        return block
    pad = jnp.zeros((abs(by),) + block.shape[1:], block.dtype)
    if by > 0:
        return jnp.concatenate([pad, block[:-by]], axis=0)
    return jnp.concatenate([block[-by:], pad], axis=0)


def deltas_of(share, p, sup, above):
    p = p.astype(F32)
    weighted = (sup.astype(F32).reshape(64, 8, C) * share[None]).reshape(VOX, C)
    grad = weighted.astype(BF16).astype(F32) + above.astype(F32)
    sig = jax.nn.sigmoid(p)
    return grad * (sig * (1.0 + p * (1.0 - sig)))


def spread(delta, pd):
    delta = delta.reshape(64, 8, C)
    place = lax.broadcasted_iota(jnp.int32, (64, 8, C), 1)
    for w in (-1, 0, 1):
        if w == 0:
            moved = delta
        elif w == 1:
            moved = jnp.where(place == 0, 0.0, pltpu.roll(delta, 1, 1))
        else:
            moved = jnp.where(place == 7, 0.0, pltpu.roll(delta, 7, 1))
        moved = moved.reshape(8, 8, 8, C)
        zero = jnp.zeros((8, 1, 8, C), F32)
        for v in (-1, 0, 1):
            if v == 0:
                out = moved
            elif v == 1:
                out = jnp.concatenate([zero, moved[:, :-1]], axis=1)
            else:
                out = jnp.concatenate([moved[:, 1:], zero], axis=1)
            at = ((v + 1) * 3 + (w + 1)) * C
            pd[:, at : at + C] = out.reshape(VOX, C).astype(BF16)


def input_grad(pd, wn):
    y = lax.dot_general(pd, wn, (((1,), (1,)), ((), ())), preferred_element_type=F32)
    gin = y[:, C : 2 * C] + shift_rows(y[:, :C], -64) + shift_rows(y[:, 2 * C :], 64)
    return gin.astype(BF16)


def working(slot):
    return lax.axis_size("section") - 1 - lax.axis_index("section") == slot // WORK


def first_kernel(c_hbm, p_hbm, sup_hbm, w_hbm, gin, deltas, gins, wn, p_ref, sup_ref, shares, *rest):
    pd, w_ref, counts, sems = rest
    active = working(0)
    later = pl.ds(1, WORK - 1)
    copies = [
        pltpu.make_async_copy(c_hbm, counts, sems.at[0]),
        pltpu.make_async_copy(p_hbm.at[0], p_ref.at[0], sems.at[1]),
        pltpu.make_async_copy(sup_hbm.at[0], sup_ref.at[0], sems.at[2]),
        pltpu.make_async_copy(w_hbm, w_ref, sems.at[3]),
        pltpu.make_async_copy(p_hbm.at[later], p_ref.at[later], sems.at[4]),
        pltpu.make_async_copy(sup_hbm.at[later], sup_ref.at[later], sems.at[5]),
    ]
    for copy in copies:
        copy.start()
    copies[0].wait()
    for brick in range(WORK):
        count = counts[brick // 2, brick % 2].astype(F32)
        shares[brick] = jnp.full((8, C), count * (1.0 / VOX), F32)
    copies[1].wait()
    copies[2].wait()

    @pl.when(active)
    def _():
        zero = jnp.zeros((VOX, C), BF16)
        delta = deltas_of(shares[0], p_ref[0], sup_ref[0], zero)
        deltas[0] = delta.astype(BF16)
        spread(delta, pd)

    copies[3].wait()
    for u in range(3):
        for tap in range(9):
            at = (u * 9 + tap) * C
            wn[u * C : (u + 1) * C, tap * C : (tap + 1) * C] = w_ref[at : at + C, :]

    @pl.when(active)
    def _():
        gin[...] = input_grad(pd[...], wn[...])
        gins[0] = gin[...]

    copies[4].wait()
    copies[5].wait()


def first_step(counts, preacts, sup, weights):
    hbm = lambda x: pltpu.with_memory_space_constraint(x, pltpu.MemorySpace.HBM)
    block, bricks = pltpu.VMEM((VOX, C), BF16), pltpu.VMEM((WORK, VOX, C), BF16)
    return pl.pallas_call(
        first_kernel,
        in_specs=[ANY] * 4,
        out_specs=[VM] * 7,
        out_shape=[
            block,
            bricks,
            bricks,
            pltpu.VMEM((3 * C, 9 * C), BF16),
            bricks,
            bricks,
            pltpu.VMEM((WORK, 8, C), F32),
        ],
        scratch_shapes=[
            pltpu.VMEM((VOX, 9 * C), BF16),
            pltpu.VMEM((TAPS * C, C), BF16),
            pltpu.SMEM((2, 2), jnp.int32),
            pltpu.SemaphoreType.DMA((6,)),
        ],
        compiler_params=params(),
        name="tick_first",
    )(hbm(counts), hbm(preacts), hbm(sup), hbm(weights))


def tick_kernel(slot, shares, p_ref, sup_ref, wn, *rest):
    deltas, gins, gin, pd = rest[-4:]
    zero = jnp.zeros((VOX, C), BF16)
    brick = slot % WORK

    @pl.when(working(slot))
    def _():
        above = zero if slot < WORK else rest[2][...]
        delta = deltas_of(shares[brick], p_ref[brick], sup_ref[brick], above)
        deltas[brick] = delta.astype(BF16)
        spread(delta, pd)
        gin[...] = input_grad(pd[...], wn[...])
        gins[brick] = gin[...]

    if slot // WORK == lax.axis_size("section") - 1:
        @pl.when(jnp.logical_not(working(slot)))
        def _():
            gin[...] = gins[brick]


def tick_step(slot, shares, preacts, sup, wn, deltas, gins, above):
    block, bricks = pltpu.VMEM((VOX, C), BF16), pltpu.VMEM((WORK, VOX, C), BF16)
    return pl.pallas_call(
        functools.partial(tick_kernel, slot),
        in_specs=[VM] * (6 + len(above)),
        out_specs=[VM] * 3,
        out_shape=[bricks, bricks, block],
        scratch_shapes=[pltpu.VMEM((VOX, 9 * C), BF16)],
        input_output_aliases={4: 0, 5: 1},
        compiler_params=params(),
        cost_estimate=pl.CostEstimate(flops=1, bytes_accessed=1 << 18, transcendentals=0),
        name="tick%d" % slot,
    )(vmem(shares), vmem(preacts), vmem(sup), vmem(wn), vmem(deltas), vmem(gins), *above)


def transpose_kernel(x_ref, out):
    for brick in range(WORK):
        x = x_ref[brick].T
        pad = jnp.zeros((C, 64), BF16)
        out[brick, :C, :] = jnp.concatenate([pad, x[:, :-64]], axis=1)
        out[brick, C : 2 * C, :] = x
        out[brick, 2 * C :, :] = jnp.concatenate([x[:, 64:], pad], axis=1)


def transpose_step(inputs):
    return pl.pallas_call(
        transpose_kernel,
        in_specs=[VM],
        out_specs=VM,
        out_shape=shape((WORK, 3 * C, VOX)),
        compiler_params=params(),
        name="inputs_across",
    )(inputs)


def early_kernel(deltas, xt, acc, pd):
    spread(deltas[0].astype(F32), pd.at[0])
    total = jnp.dot(xt[0], pd[0], preferred_element_type=F32)
    spread(deltas[1].astype(F32), pd.at[1])
    acc[...] = total + jnp.dot(xt[1], pd[1], preferred_element_type=F32)


def early_step(deltas, xt):
    return pl.pallas_call(
        early_kernel,
        in_specs=[VM] * 2,
        out_specs=VM,
        out_shape=shape((3 * C, 9 * C), F32),
        scratch_shapes=[pltpu.VMEM((2, VOX, 9 * C), BF16)],
        compiler_params=params(),
        cost_estimate=pl.CostEstimate(flops=1, bytes_accessed=1 << 18, transcendentals=0),
        name="weight_terms_early",
    )(vmem(deltas), xt)


def late_kernel(slot, shares, p_ref, sup_ref, above_ref, deltas, xt, acc_in, *rest):
    keep, send, (pd, pd_2, acc) = rest[:4], rest[4:8], rest[8:]
    active = working(slot)
    last = WORK - 1
    spread(deltas[last - 1].astype(F32), pd_2)
    total = acc_in[...] + jnp.dot(xt[last - 1], pd_2[...], preferred_element_type=F32)

    @pl.when(active)
    def _():
        spread(deltas_of(shares[last], p_ref[last], sup_ref[last], above_ref[...]), pd)

    @pl.when(jnp.logical_not(active))
    def _():
        spread(deltas[last].astype(F32), pd)

    acc[...] = total + jnp.dot(xt[last], pd[...], preferred_element_type=F32)
    me = lax.axis_index("brick")
    core, y = lax.rem(me, 2), lax.div(me, 8)
    for k in range(4):
        row = lax.bitwise_xor(y, k) * 48
        mine = pl.multiple_of(core * 192 + row, 16)
        other = pl.multiple_of((1 - core) * 192 + row, 16)
        send[k][...] = acc[pl.ds(other, 48), :].astype(BF16)
        keep[k][...] = acc[pl.ds(mine, 48), :].astype(BF16)


def late_step(slot, shares, preacts, sup, above, deltas, xt, acc):
    return pl.pallas_call(
        functools.partial(late_kernel, slot),
        in_specs=[VM] * 7,
        out_specs=[VM] * 9,
        out_shape=[shape((48, 9 * C))] * 8 + [shape((VOX, 9 * C))],
        scratch_shapes=[pltpu.VMEM((VOX, 9 * C), BF16), pltpu.VMEM((3 * C, 9 * C), F32)],
        compiler_params=params(),
        cost_estimate=pl.CostEstimate(
            flops=4 * VOX * TAPS * C * C, bytes_accessed=7 << 20, transcendentals=0
        ),
        name="weight_terms",
    )(vmem(shares), vmem(preacts), vmem(sup), above, vmem(deltas), xt, acc)


def choose(trainer, micro, owner, offset, first, second):
    peers = trainer.shape[1] // 2
    to = lax.rem(owner + offset, peers)
    first = jnp.where(trainer[micro, 2 * owner] == to, first, jnp.zeros_like(first))
    return jnp.where(trainer[micro, 2 * owner + 1] == to, second, first)


def last_kernel(slot, trainer, gins, pd, wn, gin, stays, leaves):
    active = working(slot)

    @pl.when(active)
    def _():
        gin[...] = input_grad(pd[...], wn[...])

    @pl.when(jnp.logical_not(active))
    def _():
        gin[...] = gins[WORK - 1]

    me = lax.axis_index("brick")
    core = lax.rem(me, 2)
    for micro in range(2):
        first, second = gins.at[2 * micro], gins.at[1] if micro == 0 else gin
        stays[micro] = choose(trainer, micro, me, 0, first[...], second[...])
        leaves[micro] = choose(trainer, micro, me, 1 + 2 * core, first[...], second[...])


def last_step(slot, trainer, gins, pd, wn):
    return pl.pallas_call(
        functools.partial(last_kernel, slot),
        in_specs=[SM] + [VM] * 3,
        out_specs=[VM] * 3,
        out_shape=[shape((VOX, C)), shape((2, VOX, C)), shape((2, VOX, C))],
        compiler_params=params(),
        cost_estimate=pl.CostEstimate(
            flops=2 * VOX * TAPS * C * C, bytes_accessed=4 << 20, transcendentals=0
        ),
        name="last_grad",
    )(trainer, vmem(gins), pd, vmem(wn))


def sort_kernel(trainer, *refs):
    came, keeps, passes = refs[:4], refs[4], refs[5]
    me = lax.axis_index("brick")
    core = lax.rem(me, 2)
    peers = trainer.shape[1] // 2
    owner = lax.rem(me + peers - 2, peers)
    for micro in range(2):
        first, second = came[2 * micro][...], came[2 * micro + 1][...]
        keeps[micro] = choose(trainer, micro, owner, 2, first, second)
        passes[micro] = choose(trainer, micro, owner, 3 - 2 * core, first, second)


def sort_step(trainer, came):
    return pl.pallas_call(
        sort_kernel,
        in_specs=[SM] + [VM] * 4,
        out_specs=[VM] * 2,
        out_shape=[shape((2, VOX, C))] * 2,
        compiler_params=params(),
        name="sort_slots",
    )(trainer, *came)


def slots_kernel(stays, keeps, passed, arrived, out, sems):
    core = lax.rem(lax.axis_index("brick"), 2)
    copies = [
        pltpu.make_async_copy(block.at[micro], out.at[micro, d], sems.at[i, micro])
        for i, (block, d) in enumerate(
            ((stays, 0), (keeps, 2), (passed, 1 + 2 * core), (arrived, 3 - 2 * core))
        )
        for micro in range(2)
    ]
    for copy in copies:
        copy.start()
    for copy in copies:
        copy.wait()


def slots_step(*blocks):
    return pl.pallas_call(
        slots_kernel,
        in_specs=[VM] * 4,
        out_specs=ANY,
        out_shape=shape((2, 4, VOX, C)),
        scratch_shapes=[pltpu.SemaphoreType.DMA((4, 2))],
        compiler_params=params(),
        name="slots",
    )(*blocks)


def finish_kernel(scale, mine, other, out_hbm, out, sems):
    me = lax.axis_index("brick")
    core = lax.rem(me, 2)
    label = lax.div(me, 8)
    copies = []
    for u in range(3):
        for i in range(8):
            group = u * 8 + i
            half, part, row = group // 12, group % 12 // 3, group % 3 * 16
            at = lax.bitwise_xor(label, part)
            rows = jnp.where(core == half, mine[at, row : row + 16], other[at, row : row + 16])
            rows = rows.astype(F32) * scale
            for tap in range(9):
                to = (u * 9 + tap) * C + i * 16
                out[to : to + 16, :] = rows[:, tap * C : (tap + 1) * C]
        size = 9 * C
        copies.append(
            pltpu.make_async_copy(
                out.at[u * size : (u + 1) * size], out_hbm.at[u * size : (u + 1) * size], sems.at[u]
            )
        )
        copies[-1].start()
    for copy in copies:
        copy.wait()


def finish_step(scale, mine, other):
    return pl.pallas_call(
        functools.partial(finish_kernel, scale),
        in_specs=[VM] * 2,
        out_specs=ANY,
        out_shape=shape((TAPS * C, C), F32),
        scratch_shapes=[pltpu.VMEM((TAPS * C, C), F32), pltpu.SemaphoreType.DMA((3,))],
        compiler_params=params(),
        name="finish_weights",
    )(mine, other)


def swap(block, bits):
    pairs = [(i, i ^ bits) for i in range(lax.axis_size("brick"))]
    return lax.ppermute(block, "brick", pairs)


def shifted(block, distance):
    n = lax.axis_size("brick")
    return lax.ppermute(block, "brick", [(i, (i + distance) % n) for i in range(n)])


def shards(saved_inputs, saved_preacts, supervision, weights, trainer, counts):
    peers = lax.axis_size("brick")
    me = lax.axis_index("brick")
    layers = lax.axis_size("section")
    micros, own = saved_inputs.shape[1:3]
    slots = WORK * layers

    inputs = saved_inputs.reshape(WORK, VOX, C)
    preacts = saved_preacts.reshape(WORK, VOX, C)
    sup = supervision.reshape(WORK, VOX, C)
    above, came = {}, []
    gin, deltas, gins, wn, preacts, sup, shares = first_step(counts, preacts, sup, weights[0])
    xt = transpose_step(inputs)
    for slot in range(slots - 1):
        if slot > 0:
            arrived = [above[slot]] if slot >= WORK else []
            deltas, gins, gin = tick_step(
                slot, shares, preacts, sup, wn, deltas, gins, arrived
            )
        sender = layers - 1 - slot // WORK
        if sender > 0:
            above[slot + WORK] = lax.ppermute(gin, "section", [(sender, sender - 1)])
        else:
            came.append(shifted(gin, 2))
        if slot == slots - 3:
            acc = early_step(deltas, xt)
    last = slots - 1
    *halves, pd = late_step(last, shares, preacts, sup, above[last], deltas, xt, acc)
    keep, send = halves[:4], halves[4:]
    send, came[0] = lax.optimization_barrier([send, came[0]])
    from_core = [swap(block, 1) for block in send]
    gin, stays, leaves = last_step(last, trainer, gins, pd, wn)
    from_core, gin, leaves, came[1] = lax.optimization_barrier([from_core, gin, leaves, came[1]])
    came.append(shifted(gin, 2))
    across = [(i, (i + 1 + 2 * (i % 2)) % peers) for i in range(peers)]
    arrived = lax.ppermute(leaves, "brick", across)

    part = [mine.astype(F32) + theirs.astype(F32) for mine, theirs in zip(keep, from_core)]
    total = part[0]
    for block, bits in zip(part[1:], Y_BITS):
        total = total + swap(block.astype(BF16), bits).astype(F32)
    total = total.astype(BF16)
    keeps, passes = sort_step(trainer, came)
    passed = swap(passes, 1)
    total, passed = lax.optimization_barrier([total, passed])
    full = total.astype(F32)
    for bits in Z_BITS:
        full = full + swap(total, bits).astype(F32)
    full = full.astype(BF16)
    got = [swap(full, bits) for bits in Y_BITS]
    got, arrived = lax.optimization_barrier([got, arrived])
    skip_grads = slots_step(stays, keeps, passed, arrived)
    skip_grads = skip_grads.reshape((1, micros, 4) + saved_inputs.shape[3:])
    mine = jnp.stack([full] + got)
    other = swap(mine, 1)
    scale = 1.0 / math.sqrt(WORK * peers * VOX)
    weight_grads = finish_step(scale, mine, other)
    return skip_grads, weight_grads[None]


def solution(mesh):
    bricks = P("section", None, "brick", None, None, None, None)
    in_specs = (bricks, bricks, bricks, P("section", None, None), P(), P(None, "brick"))
    out_specs = (bricks, P("section", None, None))
    return jax.shard_map(shards, mesh=mesh, in_specs=in_specs, out_specs=out_specs, check_vma=False)
```

```python
import functools
import math

import jax
import jax.numpy as jnp
from jax import lax
from jax.experimental import pallas as pl
from jax.experimental.pallas import tpu as pltpu
from jax.sharding import PartitionSpec as P

C = 128
VOX = 512
TAPS = 27
WORK = 4
F32 = jnp.float32
BF16 = jnp.bfloat16
ANY = pl.BlockSpec(memory_space=pl.ANY)
VM = pl.BlockSpec(memory_space=pltpu.VMEM)
SM = pl.BlockSpec(memory_space=pltpu.SMEM)
Y_BITS = (8, 16, 24)
Z_BITS = (2, 4, 6)


def shape(dims, dtype=BF16):
    return jax.ShapeDtypeStruct(dims, dtype)


def vmem(x):
    return pltpu.with_memory_space_constraint(x, pltpu.MemorySpace.VMEM)


def params():
    return pltpu.CompilerParams(vmem_limit_bytes=16 << 20)


def shift_rows(block, by):
    if by == 0:
        return block
    pad = jnp.zeros((abs(by),) + block.shape[1:], block.dtype)
    if by > 0:
        return jnp.concatenate([pad, block[:-by]], axis=0)
    return jnp.concatenate([block[-by:], pad], axis=0)


def deltas_of(share, p, sup, above):
    p = p.astype(F32)
    weighted = (sup.astype(F32).reshape(64, 8, C) * share[None]).reshape(VOX, C)
    grad = weighted.astype(BF16).astype(F32) + above.astype(F32)
    sig = jax.nn.sigmoid(p)
    return grad * (sig * (1.0 + p * (1.0 - sig)))


def spread(delta, pd):
    delta = delta.reshape(64, 8, C)
    place = lax.broadcasted_iota(jnp.int32, (64, 8, C), 1)
    for w in (-1, 0, 1):
        if w == 0:
            moved = delta
        elif w == 1:
            moved = jnp.where(place == 0, 0.0, pltpu.roll(delta, 1, 1))
        else:
            moved = jnp.where(place == 7, 0.0, pltpu.roll(delta, 7, 1))
        moved = moved.reshape(8, 8, 8, C)
        zero = jnp.zeros((8, 1, 8, C), F32)
        for v in (-1, 0, 1):
            if v == 0:
                out = moved
            elif v == 1:
                out = jnp.concatenate([zero, moved[:, :-1]], axis=1)
            else:
                out = jnp.concatenate([moved[:, 1:], zero], axis=1)
            at = ((v + 1) * 3 + (w + 1)) * C
            pd[:, at : at + C] = out.reshape(VOX, C).astype(BF16)


def input_grad(pd, wn):
    y = lax.dot_general(pd, wn, (((1,), (1,)), ((), ())), preferred_element_type=F32)
    gin = y[:, C : 2 * C] + shift_rows(y[:, :C], -64) + shift_rows(y[:, 2 * C :], 64)
    return gin.astype(BF16)


def working(slot):
    return lax.axis_size("section") - 1 - lax.axis_index("section") == slot // WORK


def first_kernel(c_hbm, p_hbm, sup_hbm, w_hbm, gin, deltas, gins, wn, p_ref, sup_ref, shares, *rest):
    pd, w_ref, counts, sems = rest
    active = working(0)
    later = pl.ds(1, WORK - 1)
    copies = [
        pltpu.make_async_copy(c_hbm, counts, sems.at[0]),
        pltpu.make_async_copy(p_hbm.at[0], p_ref.at[0], sems.at[1]),
        pltpu.make_async_copy(sup_hbm.at[0], sup_ref.at[0], sems.at[2]),
        pltpu.make_async_copy(w_hbm, w_ref, sems.at[3]),
        pltpu.make_async_copy(p_hbm.at[later], p_ref.at[later], sems.at[4]),
        pltpu.make_async_copy(sup_hbm.at[later], sup_ref.at[later], sems.at[5]),
    ]
    for copy in copies:
        copy.start()
    copies[0].wait()
    for brick in range(WORK):
        count = counts[brick // 2, brick % 2].astype(F32)
        shares[brick] = jnp.full((8, C), count * (1.0 / VOX), F32)
    copies[1].wait()
    copies[2].wait()

    @pl.when(active)
    def _():
        zero = jnp.zeros((VOX, C), BF16)
        delta = deltas_of(shares[0], p_ref[0], sup_ref[0], zero)
        deltas[0] = delta.astype(BF16)
        spread(delta, pd)

    copies[3].wait()
    for u in range(3):
        for tap in range(9):
            at = (u * 9 + tap) * C
            wn[u * C : (u + 1) * C, tap * C : (tap + 1) * C] = w_ref[at : at + C, :]

    @pl.when(active)
    def _():
        gin[...] = input_grad(pd[...], wn[...])
        gins[0] = gin[...]

    copies[4].wait()
    copies[5].wait()


def first_step(counts, preacts, sup, weights):
    hbm = lambda x: pltpu.with_memory_space_constraint(x, pltpu.MemorySpace.HBM)
    block, bricks = pltpu.VMEM((VOX, C), BF16), pltpu.VMEM((WORK, VOX, C), BF16)
    return pl.pallas_call(
        first_kernel,
        in_specs=[ANY] * 4,
        out_specs=[VM] * 7,
        out_shape=[
            block,
            bricks,
            bricks,
            pltpu.VMEM((3 * C, 9 * C), BF16),
            bricks,
            bricks,
            pltpu.VMEM((WORK, 8, C), F32),
        ],
        scratch_shapes=[
            pltpu.VMEM((VOX, 9 * C), BF16),
            pltpu.VMEM((TAPS * C, C), BF16),
            pltpu.SMEM((2, 2), jnp.int32),
            pltpu.SemaphoreType.DMA((6,)),
        ],
        compiler_params=params(),
        name="tick_first",
    )(hbm(counts), hbm(preacts), hbm(sup), hbm(weights))


def tick_kernel(slot, shares, p_ref, sup_ref, wn, *rest):
    deltas, gins, gin, pd = rest[-4:]
    zero = jnp.zeros((VOX, C), BF16)
    brick = slot % WORK

    @pl.when(working(slot))
    def _():
        above = zero if slot < WORK else rest[2][...]
        delta = deltas_of(shares[brick], p_ref[brick], sup_ref[brick], above)
        deltas[brick] = delta.astype(BF16)
        spread(delta, pd)
        gin[...] = input_grad(pd[...], wn[...])
        gins[brick] = gin[...]

    if slot // WORK == lax.axis_size("section") - 1:
        @pl.when(jnp.logical_not(working(slot)))
        def _():
            gin[...] = gins[brick]


def tick_step(slot, shares, preacts, sup, wn, deltas, gins, above):
    block, bricks = pltpu.VMEM((VOX, C), BF16), pltpu.VMEM((WORK, VOX, C), BF16)
    return pl.pallas_call(
        functools.partial(tick_kernel, slot),
        in_specs=[VM] * (6 + len(above)),
        out_specs=[VM] * 3,
        out_shape=[bricks, bricks, block],
        scratch_shapes=[pltpu.VMEM((VOX, 9 * C), BF16)],
        input_output_aliases={4: 0, 5: 1},
        compiler_params=params(),
        cost_estimate=pl.CostEstimate(flops=1, bytes_accessed=1 << 18, transcendentals=0),
        name="tick%d" % slot,
    )(vmem(shares), vmem(preacts), vmem(sup), vmem(wn), vmem(deltas), vmem(gins), *above)


def transpose_kernel(x_ref, out):
    for brick in range(WORK):
        x = x_ref[brick].T
        pad = jnp.zeros((C, 64), BF16)
        out[brick, :C, :] = jnp.concatenate([pad, x[:, :-64]], axis=1)
        out[brick, C : 2 * C, :] = x
        out[brick, 2 * C :, :] = jnp.concatenate([x[:, 64:], pad], axis=1)


def transpose_step(inputs):
    return pl.pallas_call(
        transpose_kernel,
        in_specs=[VM],
        out_specs=VM,
        out_shape=shape((WORK, 3 * C, VOX)),
        compiler_params=params(),
        name="inputs_across",
    )(inputs)


def early_kernel(deltas, xt, acc, pd):
    spread(deltas[0].astype(F32), pd.at[0])
    total = jnp.dot(xt[0], pd[0], preferred_element_type=F32)
    spread(deltas[1].astype(F32), pd.at[1])
    acc[...] = total + jnp.dot(xt[1], pd[1], preferred_element_type=F32)


def early_step(deltas, xt):
    return pl.pallas_call(
        early_kernel,
        in_specs=[VM] * 2,
        out_specs=VM,
        out_shape=shape((3 * C, 9 * C), F32),
        scratch_shapes=[pltpu.VMEM((2, VOX, 9 * C), BF16)],
        compiler_params=params(),
        cost_estimate=pl.CostEstimate(flops=1, bytes_accessed=1 << 18, transcendentals=0),
        name="weight_terms_early",
    )(vmem(deltas), xt)


def late_kernel(slot, shares, p_ref, sup_ref, above_ref, deltas, xt, acc_in, *rest):
    keep, send, (pd, pd_2, acc) = rest[:4], rest[4:8], rest[8:]
    active = working(slot)
    last = WORK - 1
    spread(deltas[last - 1].astype(F32), pd_2)
    total = acc_in[...] + jnp.dot(xt[last - 1], pd_2[...], preferred_element_type=F32)

    @pl.when(active)
    def _():
        spread(deltas_of(shares[last], p_ref[last], sup_ref[last], above_ref[...]), pd)

    @pl.when(jnp.logical_not(active))
    def _():
        spread(deltas[last].astype(F32), pd)

    acc[...] = total + jnp.dot(xt[last], pd[...], preferred_element_type=F32)
    me = lax.axis_index("brick")
    core, y = lax.rem(me, 2), lax.div(me, 8)
    for k in range(4):
        row = lax.bitwise_xor(y, k) * 48
        mine = pl.multiple_of(core * 192 + row, 16)
        other = pl.multiple_of((1 - core) * 192 + row, 16)
        send[k][...] = acc[pl.ds(other, 48), :].astype(BF16)
        keep[k][...] = acc[pl.ds(mine, 48), :].astype(BF16)


def late_step(slot, shares, preacts, sup, above, deltas, xt, acc):
    return pl.pallas_call(
        functools.partial(late_kernel, slot),
        in_specs=[VM] * 7,
        out_specs=[VM] * 9,
        out_shape=[shape((48, 9 * C))] * 8 + [shape((VOX, 9 * C))],
        scratch_shapes=[pltpu.VMEM((VOX, 9 * C), BF16), pltpu.VMEM((3 * C, 9 * C), F32)],
        compiler_params=params(),
        cost_estimate=pl.CostEstimate(
            flops=4 * VOX * TAPS * C * C, bytes_accessed=7 << 20, transcendentals=0
        ),
        name="weight_terms",
    )(vmem(shares), vmem(preacts), vmem(sup), above, vmem(deltas), xt, acc)


def choose(trainer, micro, owner, offset, first, second):
    peers = trainer.shape[1] // 2
    to = lax.rem(owner + offset, peers)
    first = jnp.where(trainer[micro, 2 * owner] == to, first, jnp.zeros_like(first))
    return jnp.where(trainer[micro, 2 * owner + 1] == to, second, first)


def last_kernel(slot, trainer, gins, pd, wn, gin, stays, leaves):
    active = working(slot)

    @pl.when(active)
    def _():
        gin[...] = input_grad(pd[...], wn[...])

    @pl.when(jnp.logical_not(active))
    def _():
        gin[...] = gins[WORK - 1]

    me = lax.axis_index("brick")
    core = lax.rem(me, 2)
    for micro in range(2):
        first, second = gins.at[2 * micro], gins.at[1] if micro == 0 else gin
        stays[micro] = choose(trainer, micro, me, 0, first[...], second[...])
        leaves[micro] = choose(trainer, micro, me, 1 + 2 * core, first[...], second[...])


def last_step(slot, trainer, gins, pd, wn):
    return pl.pallas_call(
        functools.partial(last_kernel, slot),
        in_specs=[SM] + [VM] * 3,
        out_specs=[VM] * 3,
        out_shape=[shape((VOX, C)), shape((2, VOX, C)), shape((2, VOX, C))],
        compiler_params=params(),
        cost_estimate=pl.CostEstimate(
            flops=2 * VOX * TAPS * C * C, bytes_accessed=4 << 20, transcendentals=0
        ),
        name="last_grad",
    )(trainer, vmem(gins), pd, vmem(wn))


def slots_kernel(trainer, stays, arrived, *refs):
    came, passed, out, keeps, passes, sems = refs[:4], refs[4:8], *refs[8:]
    me = lax.axis_index("brick")
    core = lax.rem(me, 2)
    peers = trainer.shape[1] // 2
    near = lax.rem(me + peers - 2, peers)
    far = lax.rem(me + peers - 1 - 2 * core, peers)
    copies = [
        pltpu.make_async_copy(block.at[micro], out.at[micro, d], sems.at[i, micro])
        for i, (block, d) in enumerate(
            ((stays, 0), (arrived, 3 - 2 * core), (keeps, 2), (passes, 1 + 2 * core))
        )
        for micro in range(2)
    ]
    for copy in copies[:4]:
        copy.start()
    for micro in range(2):
        bricks = slice(2 * micro, 2 * micro + 2)
        first, second = [ref[...] for ref in came[bricks]]
        keeps[micro] = choose(trainer, micro, near, 2, first, second)
        first, second = [ref[...] for ref in passed[bricks]]
        passes[micro] = choose(trainer, micro, far, 1 + 2 * core, first, second)
        copies[4 + micro].start()
        copies[6 + micro].start()
    for copy in copies:
        copy.wait()


def slots_step(trainer, stays, arrived, came, passed):
    return pl.pallas_call(
        slots_kernel,
        in_specs=[SM] + [VM] * 10,
        out_specs=ANY,
        out_shape=shape((2, 4, VOX, C)),
        scratch_shapes=[
            pltpu.VMEM((2, VOX, C), BF16),
            pltpu.VMEM((2, VOX, C), BF16),
            pltpu.SemaphoreType.DMA((4, 2)),
        ],
        compiler_params=params(),
        name="slots",
    )(trainer, stays, arrived, *came, *passed)


def finish_kernel(scale, mine, other, out_hbm, out, sems):
    me = lax.axis_index("brick")
    core = lax.rem(me, 2)
    label = lax.div(me, 8)
    copies = []
    for u in range(3):
        for i in range(8):
            group = u * 8 + i
            half, part, row = group // 12, group % 12 // 3, group % 3 * 16
            at = lax.bitwise_xor(label, part)
            rows = jnp.where(core == half, mine[at, row : row + 16], other[at, row : row + 16])
            rows = rows.astype(F32) * scale
            for tap in range(9):
                to = (u * 9 + tap) * C + i * 16
                out[to : to + 16, :] = rows[:, tap * C : (tap + 1) * C]
        size = 9 * C
        copies.append(
            pltpu.make_async_copy(
                out.at[u * size : (u + 1) * size], out_hbm.at[u * size : (u + 1) * size], sems.at[u]
            )
        )
        copies[-1].start()
    for copy in copies:
        copy.wait()


def finish_step(scale, mine, other):
    return pl.pallas_call(
        functools.partial(finish_kernel, scale),
        in_specs=[VM] * 2,
        out_specs=ANY,
        out_shape=shape((TAPS * C, C), F32),
        scratch_shapes=[pltpu.VMEM((TAPS * C, C), F32), pltpu.SemaphoreType.DMA((3,))],
        compiler_params=params(),
        name="finish_weights",
    )(mine, other)


def swap(block, bits):
    pairs = [(i, i ^ bits) for i in range(lax.axis_size("brick"))]
    return lax.ppermute(block, "brick", pairs)


def shifted(block, distance):
    n = lax.axis_size("brick")
    return lax.ppermute(block, "brick", [(i, (i + distance) % n) for i in range(n)])


def shards(saved_inputs, saved_preacts, supervision, weights, trainer, counts):
    peers = lax.axis_size("brick")
    me = lax.axis_index("brick")
    layers = lax.axis_size("section")
    micros, own = saved_inputs.shape[1:3]
    slots = WORK * layers

    inputs = saved_inputs.reshape(WORK, VOX, C)
    preacts = saved_preacts.reshape(WORK, VOX, C)
    sup = supervision.reshape(WORK, VOX, C)
    above, came = {}, []
    gin, deltas, gins, wn, preacts, sup, shares = first_step(counts, preacts, sup, weights[0])
    xt = transpose_step(inputs)
    for slot in range(slots - 1):
        if slot > 0:
            arrived = [above[slot]] if slot >= WORK else []
            deltas, gins, gin = tick_step(
                slot, shares, preacts, sup, wn, deltas, gins, arrived
            )
        sender = layers - 1 - slot // WORK
        if sender > 0:
            above[slot + WORK] = lax.ppermute(gin, "section", [(sender, sender - 1)])
        else:
            came.append(shifted(gin, 2))
        if slot == slots - 3:
            acc = early_step(deltas, xt)
    last = slots - 1
    *halves, pd = late_step(last, shares, preacts, sup, above[last], deltas, xt, acc)
    keep, send = halves[:4], halves[4:]
    send, came[0] = lax.optimization_barrier([send, came[0]])
    from_core = [swap(block, 1) for block in send]
    gin, stays, leaves = last_step(last, trainer, gins, pd, wn)
    from_core, came[1] = lax.optimization_barrier([from_core, came[1]])
    across = [(i, (i + 1 + 2 * (i % 2)) % peers) for i in range(peers)]
    arrived = lax.ppermute(leaves, "brick", across)

    part = [mine.astype(F32) + theirs.astype(F32) for mine, theirs in zip(keep, from_core)]
    total = part[0]
    for block, bits in zip(part[1:], Y_BITS):
        total = total + swap(block.astype(BF16), bits).astype(F32)
    total = total.astype(BF16)
    passed = [swap(block, 1) for block in came]
    total, passed = lax.optimization_barrier([total, passed])
    full = total.astype(F32)
    for bits in Z_BITS:
        full = full + swap(total, bits).astype(F32)
    full = full.astype(BF16)
    got = [swap(full, bits) for bits in Y_BITS]
    came.append(shifted(gin, 2))
    passed.append(swap(came[3], 1))
    got, arrived, passed = lax.optimization_barrier([got, arrived, passed])
    skip_grads = slots_step(trainer, stays, arrived, came, passed)
    skip_grads = skip_grads.reshape((1, micros, 4) + saved_inputs.shape[3:])
    mine = jnp.stack([full] + got)
    other = swap(mine, 1)
    scale = 1.0 / math.sqrt(WORK * peers * VOX)
    weight_grads = finish_step(scale, mine, other)
    return skip_grads, weight_grads[None]


def solution(mesh):
    bricks = P("section", None, "brick", None, None, None, None)
    in_specs = (bricks, bricks, bricks, P("section", None, None), P(), P(None, "brick"))
    out_specs = (bricks, P("section", None, None))
    return jax.shard_map(shards, mesh=mesh, in_specs=in_specs, out_specs=out_specs, check_vma=False)
```

```python
import functools
import math

import jax
import jax.numpy as jnp
from jax import lax
from jax.experimental import pallas as pl
from jax.experimental.pallas import tpu as pltpu
from jax.sharding import PartitionSpec as P

C = 128
VOX = 512
TAPS = 27
WORK = 4
F32 = jnp.float32
BF16 = jnp.bfloat16
ANY = pl.BlockSpec(memory_space=pl.ANY)
VM = pl.BlockSpec(memory_space=pltpu.VMEM)
SM = pl.BlockSpec(memory_space=pltpu.SMEM)
Y_BITS = (8, 16, 24)
Z_BITS = (2, 4, 6)


def shape(dims, dtype=BF16):
    return jax.ShapeDtypeStruct(dims, dtype)


def vmem(x):
    return pltpu.with_memory_space_constraint(x, pltpu.MemorySpace.VMEM)


def params():
    return pltpu.CompilerParams(vmem_limit_bytes=16 << 20)


def shift_rows(block, by):
    if by == 0:
        return block
    pad = jnp.zeros((abs(by),) + block.shape[1:], block.dtype)
    if by > 0:
        return jnp.concatenate([pad, block[:-by]], axis=0)
    return jnp.concatenate([block[-by:], pad], axis=0)


def deltas_of(share, p, sup, above):
    p = p.astype(F32)
    weighted = (sup.astype(F32).reshape(64, 8, C) * share[None]).reshape(VOX, C)
    grad = weighted.astype(BF16).astype(F32) + above.astype(F32)
    sig = jax.nn.sigmoid(p)
    return grad * (sig * (1.0 + p * (1.0 - sig)))


def spread(delta, pd):
    delta = delta.reshape(64, 8, C)
    place = lax.broadcasted_iota(jnp.int32, (64, 8, C), 1)
    for w in (-1, 0, 1):
        if w == 0:
            moved = delta
        elif w == 1:
            moved = jnp.where(place == 0, 0.0, pltpu.roll(delta, 1, 1))
        else:
            moved = jnp.where(place == 7, 0.0, pltpu.roll(delta, 7, 1))
        moved = moved.reshape(8, 8, 8, C)
        zero = jnp.zeros((8, 1, 8, C), F32)
        for v in (-1, 0, 1):
            if v == 0:
                out = moved
            elif v == 1:
                out = jnp.concatenate([zero, moved[:, :-1]], axis=1)
            else:
                out = jnp.concatenate([moved[:, 1:], zero], axis=1)
            at = ((v + 1) * 3 + (w + 1)) * C
            pd[:, at : at + C] = out.reshape(VOX, C).astype(BF16)


def input_grad(pd, wn):
    y = lax.dot_general(pd, wn, (((1,), (1,)), ((), ())), preferred_element_type=F32)
    gin = y[:, C : 2 * C] + shift_rows(y[:, :C], -64) + shift_rows(y[:, 2 * C :], 64)
    return gin.astype(BF16)


def working(slot):
    return lax.axis_size("section") - 1 - lax.axis_index("section") == slot // WORK


def first_kernel(c_hbm, p_hbm, sup_hbm, w_hbm, gin, deltas, gins, wn, p_ref, sup_ref, shares, *rest):
    pd, w_ref, counts, sems = rest
    active = working(0)
    later = pl.ds(1, WORK - 1)
    copies = [
        pltpu.make_async_copy(c_hbm, counts, sems.at[0]),
        pltpu.make_async_copy(p_hbm.at[0], p_ref.at[0], sems.at[1]),
        pltpu.make_async_copy(sup_hbm.at[0], sup_ref.at[0], sems.at[2]),
        pltpu.make_async_copy(w_hbm, w_ref, sems.at[3]),
        pltpu.make_async_copy(p_hbm.at[later], p_ref.at[later], sems.at[4]),
        pltpu.make_async_copy(sup_hbm.at[later], sup_ref.at[later], sems.at[5]),
    ]
    for copy in copies:
        copy.start()
    copies[0].wait()
    for brick in range(WORK):
        count = counts[brick // 2, brick % 2].astype(F32)
        shares[brick] = jnp.full((8, C), count * (1.0 / VOX), F32)
    copies[1].wait()
    copies[2].wait()

    @pl.when(active)
    def _():
        zero = jnp.zeros((VOX, C), BF16)
        delta = deltas_of(shares[0], p_ref[0], sup_ref[0], zero)
        deltas[0] = delta.astype(BF16)
        spread(delta, pd)

    copies[3].wait()
    for u in range(3):
        for tap in range(9):
            at = (u * 9 + tap) * C
            wn[u * C : (u + 1) * C, tap * C : (tap + 1) * C] = w_ref[at : at + C, :]

    @pl.when(active)
    def _():
        gin[...] = input_grad(pd[...], wn[...])
        gins[0] = gin[...]

    copies[4].wait()
    copies[5].wait()


def first_step(counts, preacts, sup, weights):
    hbm = lambda x: pltpu.with_memory_space_constraint(x, pltpu.MemorySpace.HBM)
    block, bricks = pltpu.VMEM((VOX, C), BF16), pltpu.VMEM((WORK, VOX, C), BF16)
    return pl.pallas_call(
        first_kernel,
        in_specs=[ANY] * 4,
        out_specs=[VM] * 7,
        out_shape=[
            block,
            bricks,
            bricks,
            pltpu.VMEM((3 * C, 9 * C), BF16),
            bricks,
            bricks,
            pltpu.VMEM((WORK, 8, C), F32),
        ],
        scratch_shapes=[
            pltpu.VMEM((VOX, 9 * C), BF16),
            pltpu.VMEM((TAPS * C, C), BF16),
            pltpu.SMEM((2, 2), jnp.int32),
            pltpu.SemaphoreType.DMA((6,)),
        ],
        compiler_params=params(),
        name="tick_first",
    )(hbm(counts), hbm(preacts), hbm(sup), hbm(weights))


def tick_kernel(slot, shares, p_ref, sup_ref, wn, *rest):
    last = slot // WORK == lax.axis_size("section") - 1
    deltas, gins, gin, pd = rest[-4:]
    zero = jnp.zeros((VOX, C), BF16)
    brick = slot % WORK

    @pl.when(working(slot))
    def _():
        above = zero if slot < WORK else rest[2][...]
        delta = deltas_of(shares[brick], p_ref[brick], sup_ref[brick], above)
        deltas[brick] = delta.astype(BF16)
        spread(delta, pd)
        gin[...] = input_grad(pd[...], wn[...])
        gins[brick] = gin[...]

    if last:
        @pl.when(jnp.logical_not(working(slot)))
        def _():
            gin[...] = gins[brick]
            spread(deltas[brick].astype(F32), pd)


def tick_step(slot, shares, preacts, sup, wn, deltas, gins, above):
    block, bricks = pltpu.VMEM((VOX, C), BF16), pltpu.VMEM((WORK, VOX, C), BF16)
    last = slot // WORK == lax.axis_size("section") - 1
    spread_deltas = pltpu.VMEM((VOX, 9 * C), BF16)
    return pl.pallas_call(
        functools.partial(tick_kernel, slot),
        in_specs=[VM] * (6 + len(above)),
        out_specs=[VM] * (3 + last),
        out_shape=[bricks, bricks, block] + [spread_deltas] * last,
        scratch_shapes=[] if last else [spread_deltas],
        input_output_aliases={4: 0, 5: 1},
        compiler_params=params(),
        cost_estimate=pl.CostEstimate(flops=1, bytes_accessed=1 << 18, transcendentals=0),
        name="tick%d" % slot,
    )(vmem(shares), vmem(preacts), vmem(sup), vmem(wn), vmem(deltas), vmem(gins), *above)


def transpose_kernel(x_ref, out):
    for brick in range(WORK):
        x = x_ref[brick].T
        pad = jnp.zeros((C, 64), BF16)
        out[brick, :C, :] = jnp.concatenate([pad, x[:, :-64]], axis=1)
        out[brick, C : 2 * C, :] = x
        out[brick, 2 * C :, :] = jnp.concatenate([x[:, 64:], pad], axis=1)


def transpose_step(inputs):
    return pl.pallas_call(
        transpose_kernel,
        in_specs=[VM],
        out_specs=VM,
        out_shape=shape((WORK, 3 * C, VOX)),
        compiler_params=params(),
        name="inputs_across",
    )(inputs)


def late_kernel(slot, shares, p_ref, sup_ref, above_ref, deltas, xt, *rest):
    pds, keep, send, (pd, acc) = rest[:3], rest[3:7], rest[7:11], rest[11:]
    active = working(slot)
    last = WORK - 1
    total = jnp.dot(xt[0], pds[0][...], preferred_element_type=F32)
    for brick in range(1, last):
        total = total + jnp.dot(xt[brick], pds[brick][...], preferred_element_type=F32)

    @pl.when(active)
    def _():
        spread(deltas_of(shares[last], p_ref[last], sup_ref[last], above_ref[...]), pd)

    @pl.when(jnp.logical_not(active))
    def _():
        spread(deltas[last].astype(F32), pd)

    acc[...] = total + jnp.dot(xt[last], pd[...], preferred_element_type=F32)
    me = lax.axis_index("brick")
    core, y = lax.rem(me, 2), lax.div(me, 8)
    for k in range(4):
        row = lax.bitwise_xor(y, k) * 48
        mine = pl.multiple_of(core * 192 + row, 16)
        other = pl.multiple_of((1 - core) * 192 + row, 16)
        send[k][...] = acc[pl.ds(other, 48), :].astype(BF16)
        keep[k][...] = acc[pl.ds(mine, 48), :].astype(BF16)


def late_step(slot, shares, preacts, sup, above, deltas, xt, pds):
    return pl.pallas_call(
        functools.partial(late_kernel, slot),
        in_specs=[VM] * 9,
        out_specs=[VM] * 9,
        out_shape=[shape((48, 9 * C))] * 8 + [shape((VOX, 9 * C))],
        scratch_shapes=[pltpu.VMEM((3 * C, 9 * C), F32)],
        compiler_params=params(),
        cost_estimate=pl.CostEstimate(
            flops=4 * VOX * TAPS * C * C, bytes_accessed=7 << 20, transcendentals=0
        ),
        name="weight_terms",
    )(vmem(shares), vmem(preacts), vmem(sup), above, vmem(deltas), xt, *pds)


def choose(trainer, micro, owner, offset, first, second):
    peers = trainer.shape[1] // 2
    to = lax.rem(owner + offset, peers)
    first = jnp.where(trainer[micro, 2 * owner] == to, first, jnp.zeros_like(first))
    return jnp.where(trainer[micro, 2 * owner + 1] == to, second, first)


def last_kernel(slot, trainer, gins, pd, wn, gin, stays, leaves):
    active = working(slot)

    @pl.when(active)
    def _():
        gin[...] = input_grad(pd[...], wn[...])

    @pl.when(jnp.logical_not(active))
    def _():
        gin[...] = gins[WORK - 1]

    me = lax.axis_index("brick")
    core = lax.rem(me, 2)
    for micro in range(2):
        first, second = gins.at[2 * micro], gins.at[1] if micro == 0 else gin
        stays[micro] = choose(trainer, micro, me, 0, first[...], second[...])
        leaves[micro] = choose(trainer, micro, me, 1 + 2 * core, first[...], second[...])


def last_step(slot, trainer, gins, pd, wn):
    return pl.pallas_call(
        functools.partial(last_kernel, slot),
        in_specs=[SM] + [VM] * 3,
        out_specs=[VM] * 3,
        out_shape=[shape((VOX, C)), shape((2, VOX, C)), shape((2, VOX, C))],
        compiler_params=params(),
        cost_estimate=pl.CostEstimate(
            flops=2 * VOX * TAPS * C * C, bytes_accessed=4 << 20, transcendentals=0
        ),
        name="last_grad",
    )(trainer, vmem(gins), pd, vmem(wn))


def slots_kernel(trainer, stays, arrived, *refs):
    came, passed, out, keeps, passes, sems = refs[:4], refs[4:8], *refs[8:]
    me = lax.axis_index("brick")
    core = lax.rem(me, 2)
    peers = trainer.shape[1] // 2
    near = lax.rem(me + peers - 2, peers)
    far = lax.rem(me + peers - 1 - 2 * core, peers)
    copies = [
        pltpu.make_async_copy(block.at[micro], out.at[micro, d], sems.at[i, micro])
        for i, (block, d) in enumerate(
            ((stays, 0), (arrived, 3 - 2 * core), (keeps, 2), (passes, 1 + 2 * core))
        )
        for micro in range(2)
    ]
    for copy in copies[:4]:
        copy.start()
    for micro in range(2):
        bricks = slice(2 * micro, 2 * micro + 2)
        first, second = [ref[...] for ref in came[bricks]]
        keeps[micro] = choose(trainer, micro, near, 2, first, second)
        first, second = [ref[...] for ref in passed[bricks]]
        passes[micro] = choose(trainer, micro, far, 1 + 2 * core, first, second)
        copies[4 + micro].start()
        copies[6 + micro].start()
    for copy in copies:
        copy.wait()


def slots_step(trainer, stays, arrived, came, passed):
    return pl.pallas_call(
        slots_kernel,
        in_specs=[SM] + [VM] * 10,
        out_specs=ANY,
        out_shape=shape((2, 4, VOX, C)),
        scratch_shapes=[
            pltpu.VMEM((2, VOX, C), BF16),
            pltpu.VMEM((2, VOX, C), BF16),
            pltpu.SemaphoreType.DMA((4, 2)),
        ],
        compiler_params=params(),
        name="slots",
    )(trainer, stays, arrived, *came, *passed)


def finish_kernel(scale, *refs):
    mine, other, (out_hbm, halves, out, sems) = refs[:4], refs[4:8], refs[8:]
    me = lax.axis_index("brick")
    core, y = lax.rem(me, 2), lax.div(me, 8)
    for k in range(4):
        at = lax.bitwise_xor(y, k)
        halves[core, at] = mine[k][...]
        halves[1 - core, at] = other[k][...]
    size = 9 * C
    copies = []
    for u in range(3):
        for i in range(8):
            group = u * 8 + i
            half, part, row = group // 12, group % 12 // 3, group % 3 * 16
            rows = halves[half, part, row : row + 16].astype(F32) * scale
            for tap in range(9):
                to = (u * 9 + tap) * C + i * 16
                out[to : to + 16, :] = rows[:, tap * C : (tap + 1) * C]
        at = slice(u * size, (u + 1) * size)
        copies.append(pltpu.make_async_copy(out.at[at], out_hbm.at[at], sems.at[u]))
        copies[-1].start()
    for copy in copies:
        copy.wait()


def finish_step(scale, mine, other):
    return pl.pallas_call(
        functools.partial(finish_kernel, scale),
        in_specs=[VM] * 8,
        out_specs=ANY,
        out_shape=shape((TAPS * C, C), F32),
        scratch_shapes=[
            pltpu.VMEM((2, 4, 48, 9 * C), BF16),
            pltpu.VMEM((TAPS * C, C), F32),
            pltpu.SemaphoreType.DMA((3,)),
        ],
        compiler_params=params(),
        name="finish_weights",
    )(*mine, *other)


def swap(block, bits):
    pairs = [(i, i ^ bits) for i in range(lax.axis_size("brick"))]
    return lax.ppermute(block, "brick", pairs)


def shifted(block, distance):
    n = lax.axis_size("brick")
    return lax.ppermute(block, "brick", [(i, (i + distance) % n) for i in range(n)])


def shards(saved_inputs, saved_preacts, supervision, weights, trainer, counts):
    peers = lax.axis_size("brick")
    me = lax.axis_index("brick")
    layers = lax.axis_size("section")
    micros, own = saved_inputs.shape[1:3]
    slots = WORK * layers

    inputs = saved_inputs.reshape(WORK, VOX, C)
    preacts = saved_preacts.reshape(WORK, VOX, C)
    sup = supervision.reshape(WORK, VOX, C)
    above, came, pds = {}, [], []
    gin, deltas, gins, wn, preacts, sup, shares = first_step(counts, preacts, sup, weights[0])
    for slot in range(slots - 1):
        if slot > 0:
            arrived = [above[slot]] if slot >= WORK else []
            if slot == WORK + 2:
                shares, xt = lax.optimization_barrier([shares, transpose_step(inputs)])
            deltas, gins, gin, *pd = tick_step(
                slot, shares, preacts, sup, wn, deltas, gins, arrived
            )
            pds += pd
        sender = layers - 1 - slot // WORK
        if sender > 0:
            above[slot + WORK] = lax.ppermute(gin, "section", [(sender, sender - 1)])
        else:
            came.append(shifted(gin, 2))
    last = slots - 1
    *halves, pd = late_step(last, shares, preacts, sup, above[last], deltas, xt, pds)
    keep, send = halves[:4], halves[4:]
    send, came[0] = lax.optimization_barrier([send, came[0]])
    from_core = [swap(block, 1) for block in send]
    gin, stays, leaves = last_step(last, trainer, gins, pd, wn)
    from_core, came[1] = lax.optimization_barrier([from_core, came[1]])
    across = [(i, (i + 1 + 2 * (i % 2)) % peers) for i in range(peers)]
    arrived = lax.ppermute(leaves, "brick", across)

    part = [mine.astype(F32) + theirs.astype(F32) for mine, theirs in zip(keep, from_core)]
    total = part[0]
    for block, bits in zip(part[1:], Y_BITS):
        total = total + swap(block.astype(BF16), bits).astype(F32)
    total = total.astype(BF16)
    passed = [swap(block, 1) for block in came]
    total, passed = lax.optimization_barrier([total, passed])
    full = total.astype(F32)
    for bits in (6, 2, 4):
        full = full + swap(total, bits).astype(F32)
    full = full.astype(BF16)
    got = [swap(full, bits) for bits in Y_BITS]
    came.append(shifted(gin, 2))
    passed.append(swap(came[3], 1))
    skip_grads = slots_step(trainer, stays, arrived, came, passed)
    got, skip_grads = lax.optimization_barrier([got, skip_grads])
    skip_grads = skip_grads.reshape((1, micros, 4) + saved_inputs.shape[3:])
    mine = [full] + got
    other = [swap(block, 1) for block in mine]
    scale = 1.0 / math.sqrt(WORK * peers * VOX)
    weight_grads = finish_step(scale, mine, other)
    return skip_grads, weight_grads[None]


def solution(mesh):
    bricks = P("section", None, "brick", None, None, None, None)
    in_specs = (bricks, bricks, bricks, P("section", None, None), P(), P(None, "brick"))
    out_specs = (bricks, P("section", None, None))
    return jax.shard_map(shards, mesh=mesh, in_specs=in_specs, out_specs=out_specs, check_vma=False)
```

```python
import functools
import math

import jax
import jax.numpy as jnp
from jax import lax
from jax.experimental import pallas as pl
from jax.experimental.pallas import tpu as pltpu
from jax.sharding import PartitionSpec as P

C = 128
VOX = 512
TAPS = 27
WORK = 4
F32 = jnp.float32
BF16 = jnp.bfloat16
ANY = pl.BlockSpec(memory_space=pl.ANY)
VM = pl.BlockSpec(memory_space=pltpu.VMEM)
SM = pl.BlockSpec(memory_space=pltpu.SMEM)
NEAR = (2, 8, 10)
FAR = (6, 24, 30)


def shape(dims, dtype=BF16):
    return jax.ShapeDtypeStruct(dims, dtype)


def vmem(x):
    return pltpu.with_memory_space_constraint(x, pltpu.MemorySpace.VMEM)


def params():
    return pltpu.CompilerParams(vmem_limit_bytes=16 << 20)


def shift_rows(block, by):
    if by == 0:
        return block
    pad = jnp.zeros((abs(by),) + block.shape[1:], block.dtype)
    if by > 0:
        return jnp.concatenate([pad, block[:-by]], axis=0)
    return jnp.concatenate([block[-by:], pad], axis=0)


def deltas_of(share, p, sup, above):
    p = p.astype(F32)
    weighted = (sup.astype(F32).reshape(64, 8, C) * share[None]).reshape(VOX, C)
    grad = weighted.astype(BF16).astype(F32) + above.astype(F32)
    sig = jax.nn.sigmoid(p)
    return grad * (sig * (1.0 + p * (1.0 - sig)))


def spread(delta, pd):
    delta = delta.reshape(64, 8, C)
    place = lax.broadcasted_iota(jnp.int32, (64, 8, C), 1)
    for w in (-1, 0, 1):
        if w == 0:
            moved = delta
        elif w == 1:
            moved = jnp.where(place == 0, 0.0, pltpu.roll(delta, 1, 1))
        else:
            moved = jnp.where(place == 7, 0.0, pltpu.roll(delta, 7, 1))
        moved = moved.reshape(8, 8, 8, C)
        zero = jnp.zeros((8, 1, 8, C), F32)
        for v in (-1, 0, 1):
            if v == 0:
                out = moved
            elif v == 1:
                out = jnp.concatenate([zero, moved[:, :-1]], axis=1)
            else:
                out = jnp.concatenate([moved[:, 1:], zero], axis=1)
            at = ((v + 1) * 3 + (w + 1)) * C
            pd[:, at : at + C] = out.reshape(VOX, C).astype(BF16)


def input_grad(pd, wn):
    y = lax.dot_general(pd, wn, (((1,), (1,)), ((), ())), preferred_element_type=F32)
    gin = y[:, C : 2 * C] + shift_rows(y[:, :C], -64) + shift_rows(y[:, 2 * C :], 64)
    return gin.astype(BF16)


def working(slot):
    return lax.axis_size("section") - 1 - lax.axis_index("section") == slot // WORK


def first_kernel(c_hbm, p_hbm, sup_hbm, w_hbm, gin, deltas, gins, wn, p_ref, sup_ref, shares, *rest):
    pd, w_ref, counts, sems = rest
    active = working(0)
    later = pl.ds(1, WORK - 1)
    copies = [
        pltpu.make_async_copy(c_hbm, counts, sems.at[0]),
        pltpu.make_async_copy(p_hbm.at[0], p_ref.at[0], sems.at[1]),
        pltpu.make_async_copy(sup_hbm.at[0], sup_ref.at[0], sems.at[2]),
        pltpu.make_async_copy(w_hbm, w_ref, sems.at[3]),
        pltpu.make_async_copy(p_hbm.at[later], p_ref.at[later], sems.at[4]),
        pltpu.make_async_copy(sup_hbm.at[later], sup_ref.at[later], sems.at[5]),
    ]
    for copy in copies:
        copy.start()
    copies[0].wait()
    for brick in range(WORK):
        count = counts[brick // 2, brick % 2].astype(F32)
        shares[brick] = jnp.full((8, C), count * (1.0 / VOX), F32)
    copies[1].wait()
    copies[2].wait()

    @pl.when(active)
    def _():
        zero = jnp.zeros((VOX, C), BF16)
        delta = deltas_of(shares[0], p_ref[0], sup_ref[0], zero)
        deltas[0] = delta.astype(BF16)
        spread(delta, pd)

    copies[3].wait()
    for u in range(3):
        for tap in range(9):
            at = (u * 9 + tap) * C
            wn[u * C : (u + 1) * C, tap * C : (tap + 1) * C] = w_ref[at : at + C, :]

    @pl.when(active)
    def _():
        gin[...] = input_grad(pd[...], wn[...])
        gins[0] = gin[...]

    copies[4].wait()
    copies[5].wait()


def first_step(counts, preacts, sup, weights):
    hbm = lambda x: pltpu.with_memory_space_constraint(x, pltpu.MemorySpace.HBM)
    block, bricks = pltpu.VMEM((VOX, C), BF16), pltpu.VMEM((WORK, VOX, C), BF16)
    return pl.pallas_call(
        first_kernel,
        in_specs=[ANY] * 4,
        out_specs=[VM] * 7,
        out_shape=[
            block,
            bricks,
            bricks,
            pltpu.VMEM((3 * C, 9 * C), BF16),
            bricks,
            bricks,
            pltpu.VMEM((WORK, 8, C), F32),
        ],
        scratch_shapes=[
            pltpu.VMEM((VOX, 9 * C), BF16),
            pltpu.VMEM((TAPS * C, C), BF16),
            pltpu.SMEM((2, 2), jnp.int32),
            pltpu.SemaphoreType.DMA((6,)),
        ],
        compiler_params=params(),
        name="tick_first",
    )(hbm(counts), hbm(preacts), hbm(sup), hbm(weights))


def tick_kernel(slot, shares, p_ref, sup_ref, wn, *rest):
    last = slot // WORK == lax.axis_size("section") - 1
    deltas, gins, gin, pd = rest[-4:]
    zero = jnp.zeros((VOX, C), BF16)
    brick = slot % WORK

    @pl.when(working(slot))
    def _():
        above = zero if slot < WORK else rest[2][...]
        delta = deltas_of(shares[brick], p_ref[brick], sup_ref[brick], above)
        deltas[brick] = delta.astype(BF16)
        spread(delta, pd)
        gin[...] = input_grad(pd[...], wn[...])
        gins[brick] = gin[...]

    if last:
        @pl.when(jnp.logical_not(working(slot)))
        def _():
            gin[...] = gins[brick]
            spread(deltas[brick].astype(F32), pd)


def tick_step(slot, shares, preacts, sup, wn, deltas, gins, above):
    block, bricks = pltpu.VMEM((VOX, C), BF16), pltpu.VMEM((WORK, VOX, C), BF16)
    last = slot // WORK == lax.axis_size("section") - 1
    spread_deltas = pltpu.VMEM((VOX, 9 * C), BF16)
    return pl.pallas_call(
        functools.partial(tick_kernel, slot),
        in_specs=[VM] * (6 + len(above)),
        out_specs=[VM] * (3 + last),
        out_shape=[bricks, bricks, block] + [spread_deltas] * last,
        scratch_shapes=[] if last else [spread_deltas],
        input_output_aliases={4: 0, 5: 1},
        compiler_params=params(),
        cost_estimate=pl.CostEstimate(flops=1, bytes_accessed=1 << 18, transcendentals=0),
        name="tick%d" % slot,
    )(vmem(shares), vmem(preacts), vmem(sup), vmem(wn), vmem(deltas), vmem(gins), *above)


def transpose_kernel(x_ref, out):
    for brick in range(WORK):
        x = x_ref[brick].T
        pad = jnp.zeros((C, 64), BF16)
        out[brick, :C, :] = jnp.concatenate([pad, x[:, :-64]], axis=1)
        out[brick, C : 2 * C, :] = x
        out[brick, 2 * C :, :] = jnp.concatenate([x[:, 64:], pad], axis=1)


def transpose_step(inputs):
    return pl.pallas_call(
        transpose_kernel,
        in_specs=[VM],
        out_specs=VM,
        out_shape=shape((WORK, 3 * C, VOX)),
        compiler_params=params(),
        name="inputs_across",
    )(inputs)


def late_kernel(slot, shares, p_ref, sup_ref, above_ref, deltas, xt, *rest):
    pds, keep, send, (pd, acc) = rest[:3], rest[3:7], rest[7:11], rest[11:]
    active = working(slot)
    last = WORK - 1
    total = jnp.dot(xt[0], pds[0][...], preferred_element_type=F32)
    for brick in range(1, last):
        total = total + jnp.dot(xt[brick], pds[brick][...], preferred_element_type=F32)

    @pl.when(active)
    def _():
        spread(deltas_of(shares[last], p_ref[last], sup_ref[last], above_ref[...]), pd)

    @pl.when(jnp.logical_not(active))
    def _():
        spread(deltas[last].astype(F32), pd)

    acc[...] = total + jnp.dot(xt[last], pd[...], preferred_element_type=F32)
    me = lax.axis_index("brick")
    core, y = lax.rem(me, 2), label_of(me)
    for k in range(4):
        row = lax.bitwise_xor(y, k) * 48
        mine = pl.multiple_of(core * 192 + row, 16)
        other = pl.multiple_of((1 - core) * 192 + row, 16)
        send[k][...] = acc[pl.ds(other, 48), :].astype(BF16)
        keep[k][...] = acc[pl.ds(mine, 48), :].astype(BF16)


def late_step(slot, shares, preacts, sup, above, deltas, xt, pds):
    return pl.pallas_call(
        functools.partial(late_kernel, slot),
        in_specs=[VM] * 9,
        out_specs=[VM] * 9,
        out_shape=[shape((48, 9 * C))] * 8 + [shape((VOX, 9 * C))],
        scratch_shapes=[pltpu.VMEM((3 * C, 9 * C), F32)],
        compiler_params=params(),
        cost_estimate=pl.CostEstimate(
            flops=4 * VOX * TAPS * C * C, bytes_accessed=7 << 20, transcendentals=0
        ),
        name="weight_terms",
    )(vmem(shares), vmem(preacts), vmem(sup), above, vmem(deltas), xt, *pds)


def choose(trainer, micro, owner, offset, first, second):
    peers = trainer.shape[1] // 2
    to = lax.rem(owner + offset, peers)
    first = jnp.where(trainer[micro, 2 * owner] == to, first, jnp.zeros_like(first))
    return jnp.where(trainer[micro, 2 * owner + 1] == to, second, first)


def last_kernel(slot, trainer, gins, pd, wn, gin, stays, leaves):
    active = working(slot)

    @pl.when(active)
    def _():
        gin[...] = input_grad(pd[...], wn[...])

    @pl.when(jnp.logical_not(active))
    def _():
        gin[...] = gins[WORK - 1]

    me = lax.axis_index("brick")
    core = lax.rem(me, 2)
    for micro in range(2):
        first, second = gins.at[2 * micro], gins.at[1] if micro == 0 else gin
        stays[micro] = choose(trainer, micro, me, 0, first[...], second[...])
        leaves[micro] = choose(trainer, micro, me, 1 + 2 * core, first[...], second[...])


def last_step(slot, trainer, gins, pd, wn):
    return pl.pallas_call(
        functools.partial(last_kernel, slot),
        in_specs=[SM] + [VM] * 3,
        out_specs=[VM] * 3,
        out_shape=[shape((VOX, C)), shape((2, VOX, C)), shape((2, VOX, C))],
        compiler_params=params(),
        cost_estimate=pl.CostEstimate(
            flops=2 * VOX * TAPS * C * C, bytes_accessed=4 << 20, transcendentals=0
        ),
        name="last_grad",
    )(trainer, vmem(gins), pd, vmem(wn))


def slots_kernel(trainer, stays, arrived, *refs):
    came, passed, out, keeps, passes, sems = refs[:4], refs[4:8], *refs[8:]
    me = lax.axis_index("brick")
    core = lax.rem(me, 2)
    peers = trainer.shape[1] // 2
    near = lax.rem(me + peers - 2, peers)
    far = lax.rem(me + peers - 1 - 2 * core, peers)
    copies = [
        pltpu.make_async_copy(block.at[micro], out.at[micro, d], sems.at[i, micro])
        for i, (block, d) in enumerate(
            ((stays, 0), (arrived, 3 - 2 * core), (keeps, 2), (passes, 1 + 2 * core))
        )
        for micro in range(2)
    ]
    for copy in copies[:4]:
        copy.start()
    for micro in range(2):
        bricks = slice(2 * micro, 2 * micro + 2)
        first, second = [ref[...] for ref in came[bricks]]
        keeps[micro] = choose(trainer, micro, near, 2, first, second)
        first, second = [ref[...] for ref in passed[bricks]]
        passes[micro] = choose(trainer, micro, far, 1 + 2 * core, first, second)
        copies[4 + micro].start()
        copies[6 + micro].start()
    for copy in copies:
        copy.wait()


def slots_step(trainer, stays, arrived, came, passed):
    return pl.pallas_call(
        slots_kernel,
        in_specs=[SM] + [VM] * 10,
        out_specs=ANY,
        out_shape=shape((2, 4, VOX, C)),
        scratch_shapes=[
            pltpu.VMEM((2, VOX, C), BF16),
            pltpu.VMEM((2, VOX, C), BF16),
            pltpu.SemaphoreType.DMA((4, 2)),
        ],
        compiler_params=params(),
        name="slots",
    )(trainer, stays, arrived, *came, *passed)


def finish_kernel(scale, *refs):
    mine, other, (out_hbm, halves, out, sems) = refs[:4], refs[4:8], refs[8:]
    me = lax.axis_index("brick")
    core, y = lax.rem(me, 2), label_of(me)
    for k in range(4):
        at = lax.bitwise_xor(y, k)
        halves[core, at] = mine[k][...]
        halves[1 - core, at] = other[k][...]
    size = 9 * C
    copies = []
    for u in range(3):
        for i in range(8):
            group = u * 8 + i
            half, part, row = group // 12, group % 12 // 3, group % 3 * 16
            rows = halves[half, part, row : row + 16].astype(F32) * scale
            for tap in range(9):
                to = (u * 9 + tap) * C + i * 16
                out[to : to + 16, :] = rows[:, tap * C : (tap + 1) * C]
        at = slice(u * size, (u + 1) * size)
        copies.append(pltpu.make_async_copy(out.at[at], out_hbm.at[at], sems.at[u]))
        copies[-1].start()
    for copy in copies:
        copy.wait()


def finish_step(scale, mine, other):
    return pl.pallas_call(
        functools.partial(finish_kernel, scale),
        in_specs=[VM] * 8,
        out_specs=ANY,
        out_shape=shape((TAPS * C, C), F32),
        scratch_shapes=[
            pltpu.VMEM((2, 4, 48, 9 * C), BF16),
            pltpu.VMEM((TAPS * C, C), F32),
            pltpu.SemaphoreType.DMA((3,)),
        ],
        compiler_params=params(),
        name="finish_weights",
    )(*mine, *other)


def label_of(me):
    z, y = lax.rem(lax.div(me, 2), 4), lax.div(me, 8)
    z, y = lax.bitwise_xor(z, lax.div(z, 2)), lax.bitwise_xor(y, lax.div(y, 2))
    return lax.rem(z, 2) + 2 * lax.rem(y, 2)


def swap(block, bits):
    pairs = [(i, i ^ bits) for i in range(lax.axis_size("brick"))]
    return lax.ppermute(block, "brick", pairs)


def shifted(block, distance):
    n = lax.axis_size("brick")
    return lax.ppermute(block, "brick", [(i, (i + distance) % n) for i in range(n)])


def shards(saved_inputs, saved_preacts, supervision, weights, trainer, counts):
    peers = lax.axis_size("brick")
    me = lax.axis_index("brick")
    layers = lax.axis_size("section")
    micros, own = saved_inputs.shape[1:3]
    slots = WORK * layers

    inputs = saved_inputs.reshape(WORK, VOX, C)
    preacts = saved_preacts.reshape(WORK, VOX, C)
    sup = supervision.reshape(WORK, VOX, C)
    above, came, pds = {}, [], []
    gin, deltas, gins, wn, preacts, sup, shares = first_step(counts, preacts, sup, weights[0])
    for slot in range(slots - 1):
        if slot > 0:
            arrived = [above[slot]] if slot >= WORK else []
            if slot == WORK + 2:
                shares, xt = lax.optimization_barrier([shares, transpose_step(inputs)])
            deltas, gins, gin, *pd = tick_step(
                slot, shares, preacts, sup, wn, deltas, gins, arrived
            )
            pds += pd
        sender = layers - 1 - slot // WORK
        if sender > 0:
            above[slot + WORK] = lax.ppermute(gin, "section", [(sender, sender - 1)])
        else:
            came.append(shifted(gin, 2))
    last = slots - 1
    *halves, pd = late_step(last, shares, preacts, sup, above[last], deltas, xt, pds)
    keep, send = halves[:4], halves[4:]
    send, came[0] = lax.optimization_barrier([send, came[0]])
    from_core = [swap(block, 1) for block in send]
    gin, stays, leaves = last_step(last, trainer, gins, pd, wn)
    from_core, came[1] = lax.optimization_barrier([from_core, came[1]])
    across = [(i, (i + 1 + 2 * (i % 2)) % peers) for i in range(peers)]
    arrived = lax.ppermute(leaves, "brick", across)

    part = [mine.astype(F32) + theirs.astype(F32) for mine, theirs in zip(keep, from_core)]
    total = part[0]
    for k in (2, 3, 1):
        block, bits = part[k], NEAR[k - 1]
        total = total + swap(block.astype(BF16), bits).astype(F32)
    total = total.astype(BF16)
    passed = [swap(block, 1) for block in came]
    total, passed = lax.optimization_barrier([total, passed])
    full = total.astype(F32)
    for bits in (24, 6, 30):
        full = full + swap(total, bits).astype(F32)
    full = full.astype(BF16)
    got = [swap(full, bits) for bits in NEAR]
    came.append(shifted(gin, 2))
    passed.append(swap(came[3], 1))
    skip_grads = slots_step(trainer, stays, arrived, came, passed)
    got, skip_grads = lax.optimization_barrier([got, skip_grads])
    skip_grads = skip_grads.reshape((1, micros, 4) + saved_inputs.shape[3:])
    mine = [full] + got
    other = [swap(block, 1) for block in mine]
    scale = 1.0 / math.sqrt(WORK * peers * VOX)
    weight_grads = finish_step(scale, mine, other)
    return skip_grads, weight_grads[None]


def solution(mesh):
    bricks = P("section", None, "brick", None, None, None, None)
    in_specs = (bricks, bricks, bricks, P("section", None, None), P(), P(None, "brick"))
    out_specs = (bricks, P("section", None, None))
    return jax.shard_map(shards, mesh=mesh, in_specs=in_specs, out_specs=out_specs, check_vma=False)
```

```python
import functools
import math

import jax
import jax.numpy as jnp
from jax import lax
from jax.experimental import pallas as pl
from jax.experimental.pallas import tpu as pltpu
from jax.sharding import PartitionSpec as P

C = 128
VOX = 512
TAPS = 27
WORK = 4
F32 = jnp.float32
BF16 = jnp.bfloat16
ANY = pl.BlockSpec(memory_space=pl.ANY)
VM = pl.BlockSpec(memory_space=pltpu.VMEM)
SM = pl.BlockSpec(memory_space=pltpu.SMEM)
NEAR = (2, 8, 10)
FAR = (6, 24, 30)


def shape(dims, dtype=BF16):
    return jax.ShapeDtypeStruct(dims, dtype)


def vmem(x):
    return pltpu.with_memory_space_constraint(x, pltpu.MemorySpace.VMEM)


def params():
    return pltpu.CompilerParams(vmem_limit_bytes=16 << 20)


def shift_rows(block, by):
    if by == 0:
        return block
    pad = jnp.zeros((abs(by),) + block.shape[1:], block.dtype)
    if by > 0:
        return jnp.concatenate([pad, block[:-by]], axis=0)
    return jnp.concatenate([block[-by:], pad], axis=0)


def deltas_of(share, p, sup, above):
    p = p.astype(F32)
    weighted = (sup.astype(F32).reshape(64, 8, C) * share[None]).reshape(VOX, C)
    grad = weighted.astype(BF16).astype(F32) + above.astype(F32)
    sig = jax.nn.sigmoid(p)
    return grad * (sig * (1.0 + p * (1.0 - sig)))


def spread(delta, pd):
    delta = delta.reshape(64, 8, C)
    place = lax.broadcasted_iota(jnp.int32, (64, 8, C), 1)
    for w in (-1, 0, 1):
        if w == 0:
            moved = delta
        elif w == 1:
            moved = jnp.where(place == 0, 0.0, pltpu.roll(delta, 1, 1))
        else:
            moved = jnp.where(place == 7, 0.0, pltpu.roll(delta, 7, 1))
        moved = moved.reshape(8, 8, 8, C)
        zero = jnp.zeros((8, 1, 8, C), F32)
        for v in (-1, 0, 1):
            if v == 0:
                out = moved
            elif v == 1:
                out = jnp.concatenate([zero, moved[:, :-1]], axis=1)
            else:
                out = jnp.concatenate([moved[:, 1:], zero], axis=1)
            at = ((v + 1) * 3 + (w + 1)) * C
            pd[:, at : at + C] = out.reshape(VOX, C).astype(BF16)


def input_grad(pd, wn):
    y = lax.dot_general(pd, wn, (((1,), (1,)), ((), ())), preferred_element_type=F32)
    gin = y[:, C : 2 * C] + shift_rows(y[:, :C], -64) + shift_rows(y[:, 2 * C :], 64)
    return gin.astype(BF16)


def working(slot):
    return lax.axis_size("section") - 1 - lax.axis_index("section") == slot // WORK


def first_kernel(c_hbm, p_hbm, sup_hbm, w_hbm, gin, deltas, gins, wn, p_ref, sup_ref, shares, *rest):
    pd, w_ref, counts, sems = rest
    active = working(0)
    later = pl.ds(1, WORK - 1)
    copies = [
        pltpu.make_async_copy(c_hbm, counts, sems.at[0]),
        pltpu.make_async_copy(p_hbm.at[0], p_ref.at[0], sems.at[1]),
        pltpu.make_async_copy(sup_hbm.at[0], sup_ref.at[0], sems.at[2]),
        pltpu.make_async_copy(w_hbm, w_ref, sems.at[3]),
        pltpu.make_async_copy(p_hbm.at[later], p_ref.at[later], sems.at[4]),
        pltpu.make_async_copy(sup_hbm.at[later], sup_ref.at[later], sems.at[5]),
    ]
    for copy in copies:
        copy.start()
    copies[0].wait()
    for brick in range(WORK):
        count = counts[brick // 2, brick % 2].astype(F32)
        shares[brick] = jnp.full((8, C), count * (1.0 / VOX), F32)
    copies[1].wait()
    copies[2].wait()

    @pl.when(active)
    def _():
        zero = jnp.zeros((VOX, C), BF16)
        delta = deltas_of(shares[0], p_ref[0], sup_ref[0], zero)
        deltas[0] = delta.astype(BF16)
        spread(delta, pd)

    copies[3].wait()
    for u in range(3):
        for tap in range(9):
            at = (u * 9 + tap) * C
            wn[u * C : (u + 1) * C, tap * C : (tap + 1) * C] = w_ref[at : at + C, :]

    @pl.when(active)
    def _():
        gin[...] = input_grad(pd[...], wn[...])
        gins[0] = gin[...]

    copies[4].wait()
    copies[5].wait()


def first_step(counts, preacts, sup, weights):
    hbm = lambda x: pltpu.with_memory_space_constraint(x, pltpu.MemorySpace.HBM)
    block, bricks = pltpu.VMEM((VOX, C), BF16), pltpu.VMEM((WORK, VOX, C), BF16)
    return pl.pallas_call(
        first_kernel,
        in_specs=[ANY] * 4,
        out_specs=[VM] * 7,
        out_shape=[
            block,
            bricks,
            bricks,
            pltpu.VMEM((3 * C, 9 * C), BF16),
            bricks,
            bricks,
            pltpu.VMEM((WORK, 8, C), F32),
        ],
        scratch_shapes=[
            pltpu.VMEM((VOX, 9 * C), BF16),
            pltpu.VMEM((TAPS * C, C), BF16),
            pltpu.SMEM((2, 2), jnp.int32),
            pltpu.SemaphoreType.DMA((6,)),
        ],
        compiler_params=params(),
        name="tick_first",
    )(hbm(counts), hbm(preacts), hbm(sup), hbm(weights))


def tick_kernel(slot, shares, p_ref, sup_ref, wn, *rest):
    last = slot // WORK == lax.axis_size("section") - 1
    deltas, gins, gin, pd = rest[-4:]
    zero = jnp.zeros((VOX, C), BF16)
    brick = slot % WORK

    @pl.when(working(slot))
    def _():
        above = zero if slot < WORK else rest[2][...]
        delta = deltas_of(shares[brick], p_ref[brick], sup_ref[brick], above)
        deltas[brick] = delta.astype(BF16)
        spread(delta, pd)
        gin[...] = input_grad(pd[...], wn[...])
        gins[brick] = gin[...]

    if last:
        @pl.when(jnp.logical_not(working(slot)))
        def _():
            gin[...] = gins[brick]
            spread(deltas[brick].astype(F32), pd)


def tick_step(slot, shares, preacts, sup, wn, deltas, gins, above):
    block, bricks = pltpu.VMEM((VOX, C), BF16), pltpu.VMEM((WORK, VOX, C), BF16)
    last = slot // WORK == lax.axis_size("section") - 1
    spread_deltas = pltpu.VMEM((VOX, 9 * C), BF16)
    return pl.pallas_call(
        functools.partial(tick_kernel, slot),
        in_specs=[VM] * (6 + len(above)),
        out_specs=[VM] * (3 + last),
        out_shape=[bricks, bricks, block] + [spread_deltas] * last,
        scratch_shapes=[] if last else [spread_deltas],
        input_output_aliases={4: 0, 5: 1},
        compiler_params=params(),
        cost_estimate=pl.CostEstimate(flops=1, bytes_accessed=1 << 18, transcendentals=0),
        name="tick%d" % slot,
    )(vmem(shares), vmem(preacts), vmem(sup), vmem(wn), vmem(deltas), vmem(gins), *above)


def transpose_kernel(x_ref, out):
    for brick in range(WORK):
        x = x_ref[brick].T
        pad = jnp.zeros((C, 64), BF16)
        out[brick, :C, :] = jnp.concatenate([pad, x[:, :-64]], axis=1)
        out[brick, C : 2 * C, :] = x
        out[brick, 2 * C :, :] = jnp.concatenate([x[:, 64:], pad], axis=1)


def transpose_step(inputs):
    return pl.pallas_call(
        transpose_kernel,
        in_specs=[VM],
        out_specs=VM,
        out_shape=shape((WORK, 3 * C, VOX)),
        compiler_params=params(),
        name="inputs_across",
    )(inputs)


def late_kernel(slot, shares, p_ref, sup_ref, above_ref, deltas, xt, *rest):
    pds, keep, send, (pd, acc) = rest[:3], rest[3:7], rest[7:11], rest[11:]
    active = working(slot)
    last = WORK - 1
    total = jnp.dot(xt[0], pds[0][...], preferred_element_type=F32)
    for brick in range(1, last):
        total = total + jnp.dot(xt[brick], pds[brick][...], preferred_element_type=F32)

    @pl.when(active)
    def _():
        spread(deltas_of(shares[last], p_ref[last], sup_ref[last], above_ref[...]), pd)

    @pl.when(jnp.logical_not(active))
    def _():
        spread(deltas[last].astype(F32), pd)

    acc[...] = total + jnp.dot(xt[last], pd[...], preferred_element_type=F32)
    me = lax.axis_index("brick")
    core, y = lax.rem(me, 2), label_of(me)
    for k in range(4):
        row = lax.bitwise_xor(y, k) * 48
        mine = pl.multiple_of(core * 192 + row, 16)
        other = pl.multiple_of((1 - core) * 192 + row, 16)
        send[k][...] = acc[pl.ds(other, 48), :].astype(BF16)
        keep[k][...] = acc[pl.ds(mine, 48), :].astype(BF16)


def late_step(slot, shares, preacts, sup, above, deltas, xt, pds):
    return pl.pallas_call(
        functools.partial(late_kernel, slot),
        in_specs=[VM] * 9,
        out_specs=[VM] * 9,
        out_shape=[shape((48, 9 * C))] * 8 + [shape((VOX, 9 * C))],
        scratch_shapes=[pltpu.VMEM((3 * C, 9 * C), F32)],
        compiler_params=params(),
        cost_estimate=pl.CostEstimate(
            flops=4 * VOX * TAPS * C * C, bytes_accessed=7 << 20, transcendentals=0
        ),
        name="weight_terms",
    )(vmem(shares), vmem(preacts), vmem(sup), above, vmem(deltas), xt, *pds)


def choose(trainer, micro, owner, offset, first, second):
    peers = trainer.shape[1] // 2
    to = lax.rem(owner + offset, peers)
    first = jnp.where(trainer[micro, 2 * owner] == to, first, jnp.zeros_like(first))
    return jnp.where(trainer[micro, 2 * owner + 1] == to, second, first)


def last_kernel(slot, trainer, gins, pd, wn, gin, stays, leaves):
    active = working(slot)

    @pl.when(active)
    def _():
        gin[...] = input_grad(pd[...], wn[...])

    @pl.when(jnp.logical_not(active))
    def _():
        gin[...] = gins[WORK - 1]

    me = lax.axis_index("brick")
    core = lax.rem(me, 2)
    for micro in range(2):
        first, second = gins.at[2 * micro], gins.at[1] if micro == 0 else gin
        stays[micro] = choose(trainer, micro, me, 0, first[...], second[...])
        leaves[micro] = choose(trainer, micro, me, 1 + 2 * core, first[...], second[...])


def last_step(slot, trainer, gins, pd, wn):
    return pl.pallas_call(
        functools.partial(last_kernel, slot),
        in_specs=[SM] + [VM] * 3,
        out_specs=[VM] * 3,
        out_shape=[shape((VOX, C)), shape((2, VOX, C)), shape((2, VOX, C))],
        compiler_params=params(),
        cost_estimate=pl.CostEstimate(
            flops=2 * VOX * TAPS * C * C, bytes_accessed=4 << 20, transcendentals=0
        ),
        name="last_grad",
    )(trainer, vmem(gins), pd, vmem(wn))


def slots_kernel(trainer, stays, arrived, *refs):
    came, passed, out, keeps, passes, sems = refs[:4], refs[4:8], *refs[8:]
    me = lax.axis_index("brick")
    core = lax.rem(me, 2)
    peers = trainer.shape[1] // 2
    near = lax.rem(me + peers - 2, peers)
    far = lax.rem(me + peers - 1 - 2 * core, peers)
    copies = [
        pltpu.make_async_copy(block.at[micro], out.at[micro, d], sems.at[i, micro])
        for i, (block, d) in enumerate(
            ((stays, 0), (arrived, 3 - 2 * core), (keeps, 2), (passes, 1 + 2 * core))
        )
        for micro in range(2)
    ]
    for copy in copies[:4]:
        copy.start()
    for micro in range(2):
        bricks = slice(2 * micro, 2 * micro + 2)
        first, second = [ref[...] for ref in came[bricks]]
        keeps[micro] = choose(trainer, micro, near, 2, first, second)
        first, second = [ref[...] for ref in passed[bricks]]
        passes[micro] = choose(trainer, micro, far, 1 + 2 * core, first, second)
        copies[4 + micro].start()
        copies[6 + micro].start()
    for copy in copies:
        copy.wait()


def slots_step(trainer, stays, arrived, came, passed):
    return pl.pallas_call(
        slots_kernel,
        in_specs=[SM] + [VM] * 10,
        out_specs=ANY,
        out_shape=shape((2, 4, VOX, C)),
        scratch_shapes=[
            pltpu.VMEM((2, VOX, C), BF16),
            pltpu.VMEM((2, VOX, C), BF16),
            pltpu.SemaphoreType.DMA((4, 2)),
        ],
        compiler_params=params(),
        name="slots",
    )(trainer, stays, arrived, *came, *passed)


def finish_kernel(scale, other, *refs):
    pieces, (out_hbm, rows, whole, parts, sems) = refs[:4], refs[-5:]
    me = lax.axis_index("brick")
    core, label = lax.rem(me, 2), label_of(me)
    half = 1 - core if other else core
    for k in range(4):
        at = pl.multiple_of(lax.bitwise_xor(label, k) * 48, 16)
        rows[pl.ds(at, 48), :] = pieces[k][...]
    size = 9 * C
    to = pl.multiple_of(2 * half * size, size)
    copies = [pltpu.make_async_copy(whole, out_hbm.at[pl.ds(to, size)], sems.at[9])]
    for i in range(8):
        block = rows[pl.ds(pl.multiple_of((i + 4 * half) * 16, 16), 16), :].astype(F32) * scale
        for tap in range(9):
            at = tap * C + i * 16
            whole[at : at + 16, :] = block[:, tap * C : (tap + 1) * C]
    copies[0].start()
    for i in range(4):
        at = pl.multiple_of((i + 8 - 8 * half) * 16, 16)
        block = rows[pl.ds(at, 16), :].astype(F32) * scale
        for tap in range(9):
            parts[tap, i * 16 : (i + 1) * 16, :] = block[:, tap * C : (tap + 1) * C]
    for tap in range(9):
        to = pl.multiple_of(size + tap * C + half * 64, 64)
        copies.append(
            pltpu.make_async_copy(parts.at[tap], out_hbm.at[pl.ds(to, 64)], sems.at[tap])
        )
        copies[-1].start()
    for copy in copies:
        copy.wait()


def finish_step(scale, pieces, before=None):
    other = before is not None
    return pl.pallas_call(
        functools.partial(finish_kernel, scale, other),
        in_specs=[VM] * 4 + [ANY] * other,
        out_specs=ANY,
        out_shape=shape((TAPS * C, C), F32),
        scratch_shapes=[
            pltpu.VMEM((192, 9 * C), BF16),
            pltpu.VMEM((9 * C, C), F32),
            pltpu.VMEM((9, 64, C), F32),
            pltpu.SemaphoreType.DMA((10,)),
        ],
        input_output_aliases={4: 0} if other else {},
        compiler_params=params(),
        name="finish_other" if other else "finish_own",
    )(*pieces, *([before] if other else []))


def label_of(me):
    z, y = lax.rem(lax.div(me, 2), 4), lax.div(me, 8)
    z, y = lax.bitwise_xor(z, lax.div(z, 2)), lax.bitwise_xor(y, lax.div(y, 2))
    return lax.rem(z, 2) + 2 * lax.rem(y, 2)


def swap(block, bits):
    pairs = [(i, i ^ bits) for i in range(lax.axis_size("brick"))]
    return lax.ppermute(block, "brick", pairs)


def shifted(block, distance):
    n = lax.axis_size("brick")
    return lax.ppermute(block, "brick", [(i, (i + distance) % n) for i in range(n)])


def shards(saved_inputs, saved_preacts, supervision, weights, trainer, counts):
    peers = lax.axis_size("brick")
    me = lax.axis_index("brick")
    layers = lax.axis_size("section")
    micros, own = saved_inputs.shape[1:3]
    slots = WORK * layers

    inputs = saved_inputs.reshape(WORK, VOX, C)
    preacts = saved_preacts.reshape(WORK, VOX, C)
    sup = supervision.reshape(WORK, VOX, C)
    above, came, pds = {}, [], []
    gin, deltas, gins, wn, preacts, sup, shares = first_step(counts, preacts, sup, weights[0])
    for slot in range(slots - 1):
        if slot > 0:
            arrived = [above[slot]] if slot >= WORK else []
            if slot == WORK + 2:
                shares, xt = lax.optimization_barrier([shares, transpose_step(inputs)])
            deltas, gins, gin, *pd = tick_step(
                slot, shares, preacts, sup, wn, deltas, gins, arrived
            )
            pds += pd
        sender = layers - 1 - slot // WORK
        if sender > 0:
            above[slot + WORK] = lax.ppermute(gin, "section", [(sender, sender - 1)])
        else:
            came.append(shifted(gin, 2))
    last = slots - 1
    *halves, pd = late_step(last, shares, preacts, sup, above[last], deltas, xt, pds)
    keep, send = halves[:4], halves[4:]
    send, came[0] = lax.optimization_barrier([send, came[0]])
    from_core = [swap(block, 1) for block in send]
    gin, stays, leaves = last_step(last, trainer, gins, pd, wn)
    from_core, came[1] = lax.optimization_barrier([from_core, came[1]])
    across = [(i, (i + 1 + 2 * (i % 2)) % peers) for i in range(peers)]
    arrived = lax.ppermute(leaves, "brick", across)

    part = [mine.astype(F32) + theirs.astype(F32) for mine, theirs in zip(keep, from_core)]
    total = part[0]
    for k in (2, 3, 1):
        block, bits = part[k], NEAR[k - 1]
        total = total + swap(block.astype(BF16), bits).astype(F32)
    total = total.astype(BF16)
    passed = [swap(block, 1) for block in came]
    total, passed = lax.optimization_barrier([total, passed])
    full = total.astype(F32)
    for bits in (24, 30, 6):
        full = full + swap(total, bits).astype(F32)
    full = full.astype(BF16)
    late = {bits: swap(full, bits) for bits in (8, 2, 10)}
    got = [late[bits] for bits in NEAR]
    came.append(shifted(gin, 2))
    passed.append(swap(came[3], 1))
    skip_grads = slots_step(trainer, stays, arrived, came, passed)
    got, skip_grads = lax.optimization_barrier([got, skip_grads])
    skip_grads = skip_grads.reshape((1, micros, 4) + saved_inputs.shape[3:])
    mine = [full] + got
    other = [swap(block, 1) for block in mine]
    scale = 1.0 / math.sqrt(WORK * peers * VOX)
    weight_grads = finish_step(scale, other, finish_step(scale, mine))
    return skip_grads, weight_grads[None]


def solution(mesh):
    bricks = P("section", None, "brick", None, None, None, None)
    in_specs = (bricks, bricks, bricks, P("section", None, None), P(), P(None, "brick"))
    out_specs = (bricks, P("section", None, None))
    return jax.shard_map(shards, mesh=mesh, in_specs=in_specs, out_specs=out_specs, check_vma=False)
```

```python
import functools
import math

import jax
import jax.numpy as jnp
from jax import lax
from jax.experimental import pallas as pl
from jax.experimental.pallas import tpu as pltpu
from jax.sharding import PartitionSpec as P

C = 128
VOX = 512
TAPS = 27
WORK = 4
F32 = jnp.float32
BF16 = jnp.bfloat16
ANY = pl.BlockSpec(memory_space=pl.ANY)
VM = pl.BlockSpec(memory_space=pltpu.VMEM)
SM = pl.BlockSpec(memory_space=pltpu.SMEM)
NEAR = (2, 8, 10)
FAR = (6, 24, 30)


def shape(dims, dtype=BF16):
    return jax.ShapeDtypeStruct(dims, dtype)


def vmem(x):
    return pltpu.with_memory_space_constraint(x, pltpu.MemorySpace.VMEM)


def params():
    return pltpu.CompilerParams(vmem_limit_bytes=16 << 20)


def shift_rows(block, by):
    if by == 0:
        return block
    pad = jnp.zeros((abs(by),) + block.shape[1:], block.dtype)
    if by > 0:
        return jnp.concatenate([pad, block[:-by]], axis=0)
    return jnp.concatenate([block[-by:], pad], axis=0)


def deltas_of(share, p, sup, above):
    p = p.astype(F32)
    weighted = (sup.astype(F32).reshape(64, 8, C) * share[None]).reshape(VOX, C)
    grad = weighted.astype(BF16).astype(F32) + above.astype(F32)
    sig = jax.nn.sigmoid(p)
    return grad * (sig * (1.0 + p * (1.0 - sig)))


def spread(delta, pd):
    delta = delta.reshape(64, 8, C)
    place = lax.broadcasted_iota(jnp.int32, (64, 8, C), 1)
    for w in (-1, 0, 1):
        if w == 0:
            moved = delta
        elif w == 1:
            moved = jnp.where(place == 0, 0.0, pltpu.roll(delta, 1, 1))
        else:
            moved = jnp.where(place == 7, 0.0, pltpu.roll(delta, 7, 1))
        moved = moved.reshape(8, 8, 8, C)
        zero = jnp.zeros((8, 1, 8, C), F32)
        for v in (-1, 0, 1):
            if v == 0:
                out = moved
            elif v == 1:
                out = jnp.concatenate([zero, moved[:, :-1]], axis=1)
            else:
                out = jnp.concatenate([moved[:, 1:], zero], axis=1)
            at = ((v + 1) * 3 + (w + 1)) * C
            pd[:, at : at + C] = out.reshape(VOX, C).astype(BF16)


def input_grad(pd, wn):
    y = lax.dot_general(pd, wn, (((1,), (1,)), ((), ())), preferred_element_type=F32)
    gin = y[:, C : 2 * C] + shift_rows(y[:, :C], -64) + shift_rows(y[:, 2 * C :], 64)
    return gin.astype(BF16)


def working(slot):
    return lax.axis_size("section") - 1 - lax.axis_index("section") == slot // WORK


def first_kernel(c_hbm, p_hbm, sup_hbm, w_hbm, gin, deltas, gins, wn, p_ref, sup_ref, shares, *rest):
    pd, w_ref, counts, sems = rest
    active = working(0)
    later = pl.ds(1, WORK - 1)
    copies = [
        pltpu.make_async_copy(c_hbm, counts, sems.at[0]),
        pltpu.make_async_copy(p_hbm.at[0], p_ref.at[0], sems.at[1]),
        pltpu.make_async_copy(sup_hbm.at[0], sup_ref.at[0], sems.at[2]),
        pltpu.make_async_copy(w_hbm, w_ref, sems.at[3]),
        pltpu.make_async_copy(p_hbm.at[later], p_ref.at[later], sems.at[4]),
        pltpu.make_async_copy(sup_hbm.at[later], sup_ref.at[later], sems.at[5]),
    ]
    for copy in copies:
        copy.start()
    copies[0].wait()
    for brick in range(WORK):
        count = counts[brick // 2, brick % 2].astype(F32)
        shares[brick] = jnp.full((8, C), count * (1.0 / VOX), F32)
    copies[1].wait()
    copies[2].wait()

    @pl.when(active)
    def _():
        zero = jnp.zeros((VOX, C), BF16)
        delta = deltas_of(shares[0], p_ref[0], sup_ref[0], zero)
        deltas[0] = delta.astype(BF16)
        spread(delta, pd)

    copies[3].wait()
    for u in range(3):
        for tap in range(9):
            at = (u * 9 + tap) * C
            wn[u * C : (u + 1) * C, tap * C : (tap + 1) * C] = w_ref[at : at + C, :]

    @pl.when(active)
    def _():
        gin[...] = input_grad(pd[...], wn[...])
        gins[0] = gin[...]

    copies[4].wait()
    copies[5].wait()


def first_step(counts, preacts, sup, weights):
    hbm = lambda x: pltpu.with_memory_space_constraint(x, pltpu.MemorySpace.HBM)
    block, bricks = pltpu.VMEM((VOX, C), BF16), pltpu.VMEM((WORK, VOX, C), BF16)
    return pl.pallas_call(
        first_kernel,
        in_specs=[ANY] * 4,
        out_specs=[VM] * 7,
        out_shape=[
            block,
            bricks,
            bricks,
            pltpu.VMEM((3 * C, 9 * C), BF16),
            bricks,
            bricks,
            pltpu.VMEM((WORK, 8, C), F32),
        ],
        scratch_shapes=[
            pltpu.VMEM((VOX, 9 * C), BF16),
            pltpu.VMEM((TAPS * C, C), BF16),
            pltpu.SMEM((2, 2), jnp.int32),
            pltpu.SemaphoreType.DMA((6,)),
        ],
        compiler_params=params(),
        name="tick_first",
    )(hbm(counts), hbm(preacts), hbm(sup), hbm(weights))


def tick_kernel(slot, shares, p_ref, sup_ref, wn, *rest):
    last = slot // WORK == lax.axis_size("section") - 1
    deltas, gins, gin, pd = rest[-4:]
    zero = jnp.zeros((VOX, C), BF16)
    brick = slot % WORK

    @pl.when(working(slot))
    def _():
        above = zero if slot < WORK else rest[2][...]
        delta = deltas_of(shares[brick], p_ref[brick], sup_ref[brick], above)
        deltas[brick] = delta.astype(BF16)
        spread(delta, pd)
        gin[...] = input_grad(pd[...], wn[...])
        gins[brick] = gin[...]

    if last:
        @pl.when(jnp.logical_not(working(slot)))
        def _():
            gin[...] = gins[brick]
            spread(deltas[brick].astype(F32), pd)


def tick_step(slot, shares, preacts, sup, wn, deltas, gins, above):
    block, bricks = pltpu.VMEM((VOX, C), BF16), pltpu.VMEM((WORK, VOX, C), BF16)
    last = slot // WORK == lax.axis_size("section") - 1
    spread_deltas = pltpu.VMEM((VOX, 9 * C), BF16)
    return pl.pallas_call(
        functools.partial(tick_kernel, slot),
        in_specs=[VM] * (6 + len(above)),
        out_specs=[VM] * (3 + last),
        out_shape=[bricks, bricks, block] + [spread_deltas] * last,
        scratch_shapes=[] if last else [spread_deltas],
        input_output_aliases={4: 0, 5: 1},
        compiler_params=params(),
        cost_estimate=pl.CostEstimate(flops=1, bytes_accessed=1 << 18, transcendentals=0),
        name="tick%d" % slot,
    )(vmem(shares), vmem(preacts), vmem(sup), vmem(wn), vmem(deltas), vmem(gins), *above)


def transpose_kernel(x_ref, out):
    for brick in range(WORK):
        x = x_ref[brick].T
        pad = jnp.zeros((C, 64), BF16)
        out[brick, :C, :] = jnp.concatenate([pad, x[:, :-64]], axis=1)
        out[brick, C : 2 * C, :] = x
        out[brick, 2 * C :, :] = jnp.concatenate([x[:, 64:], pad], axis=1)


def transpose_step(inputs):
    return pl.pallas_call(
        transpose_kernel,
        in_specs=[VM],
        out_specs=VM,
        out_shape=shape((WORK, 3 * C, VOX)),
        compiler_params=params(),
        name="inputs_across",
    )(inputs)


def late_kernel(slot, shares, p_ref, sup_ref, above_ref, deltas, xt, *rest):
    pds, keep, send, (pd, acc) = rest[:3], rest[3:7], rest[7:11], rest[11:]
    active = working(slot)
    last = WORK - 1
    total = jnp.dot(xt[0], pds[0][...], preferred_element_type=F32)
    for brick in range(1, last):
        total = total + jnp.dot(xt[brick], pds[brick][...], preferred_element_type=F32)

    @pl.when(active)
    def _():
        spread(deltas_of(shares[last], p_ref[last], sup_ref[last], above_ref[...]), pd)

    @pl.when(jnp.logical_not(active))
    def _():
        spread(deltas[last].astype(F32), pd)

    acc[...] = total + jnp.dot(xt[last], pd[...], preferred_element_type=F32)
    me = lax.axis_index("brick")
    core, y = lax.rem(me, 2), label_of(me)
    for k in range(4):
        row = lax.bitwise_xor(y, k) * 48
        mine = pl.multiple_of(core * 192 + row, 16)
        other = pl.multiple_of((1 - core) * 192 + row, 16)
        send[k][...] = acc[pl.ds(other, 48), :].astype(BF16)
        keep[k][...] = acc[pl.ds(mine, 48), :].astype(BF16)


def late_step(slot, shares, preacts, sup, above, deltas, xt, pds):
    return pl.pallas_call(
        functools.partial(late_kernel, slot),
        in_specs=[VM] * 9,
        out_specs=[VM] * 9,
        out_shape=[shape((48, 9 * C))] * 8 + [shape((VOX, 9 * C))],
        scratch_shapes=[pltpu.VMEM((3 * C, 9 * C), F32)],
        compiler_params=params(),
        cost_estimate=pl.CostEstimate(
            flops=4 * VOX * TAPS * C * C, bytes_accessed=7 << 20, transcendentals=0
        ),
        name="weight_terms",
    )(vmem(shares), vmem(preacts), vmem(sup), above, vmem(deltas), xt, *pds)


def choose(trainer, micro, owner, offset, first, second):
    peers = trainer.shape[1] // 2
    to = lax.rem(owner + offset, peers)
    first = jnp.where(trainer[micro, 2 * owner] == to, first, jnp.zeros_like(first))
    return jnp.where(trainer[micro, 2 * owner + 1] == to, second, first)


def last_kernel(slot, gins, pd, wn, gin):
    @pl.when(working(slot))
    def _():
        gin[...] = input_grad(pd[...], wn[...])

    @pl.when(jnp.logical_not(working(slot)))
    def _():
        gin[...] = gins[WORK - 1]


def last_step(slot, gins, pd, wn):
    return pl.pallas_call(
        functools.partial(last_kernel, slot),
        in_specs=[VM] * 3,
        out_specs=VM,
        out_shape=shape((VOX, C)),
        compiler_params=params(),
        cost_estimate=pl.CostEstimate(
            flops=2 * VOX * TAPS * C * C, bytes_accessed=4 << 20, transcendentals=0
        ),
        name="last_grad",
    )(vmem(gins), pd, vmem(wn))


def select_kernel(trainer, gins, gin, stays, leaves):
    me = lax.axis_index("brick")
    core = lax.rem(me, 2)
    for micro in range(2):
        first = gins[2 * micro]
        second = gins[1] if micro == 0 else gin[...]
        stays[micro] = choose(trainer, micro, me, 0, first, second)
        leaves[micro] = choose(trainer, micro, me, 1 + 2 * core, first, second)


def select_step(trainer, gins, gin):
    return pl.pallas_call(
        select_kernel,
        in_specs=[SM] + [VM] * 2,
        out_specs=[VM] * 2,
        out_shape=[shape((2, VOX, C))] * 2,
        compiler_params=params(),
        cost_estimate=pl.CostEstimate(flops=1, bytes_accessed=1 << 20, transcendentals=0),
        name="select",
    )(trainer, vmem(gins), gin)


def slots_kernel(trainer, stays, arrived, *refs):
    came, passed, out, keeps, passes, sems = refs[:4], refs[4:8], *refs[8:]
    me = lax.axis_index("brick")
    core = lax.rem(me, 2)
    peers = trainer.shape[1] // 2
    near = lax.rem(me + peers - 2, peers)
    far = lax.rem(me + peers - 1 - 2 * core, peers)
    copies = [
        pltpu.make_async_copy(block.at[micro], out.at[micro, d], sems.at[i, micro])
        for i, (block, d) in enumerate(
            ((stays, 0), (arrived, 3 - 2 * core), (keeps, 2), (passes, 1 + 2 * core))
        )
        for micro in range(2)
    ]
    for copy in copies[:4]:
        copy.start()
    for micro in range(2):
        bricks = slice(2 * micro, 2 * micro + 2)
        first, second = [ref[...] for ref in came[bricks]]
        keeps[micro] = choose(trainer, micro, near, 2, first, second)
        first, second = [ref[...] for ref in passed[bricks]]
        passes[micro] = choose(trainer, micro, far, 1 + 2 * core, first, second)
        copies[4 + micro].start()
        copies[6 + micro].start()
    for copy in copies:
        copy.wait()


def slots_step(trainer, stays, arrived, came, passed):
    return pl.pallas_call(
        slots_kernel,
        in_specs=[SM] + [VM] * 10,
        out_specs=ANY,
        out_shape=shape((2, 4, VOX, C)),
        scratch_shapes=[
            pltpu.VMEM((2, VOX, C), BF16),
            pltpu.VMEM((2, VOX, C), BF16),
            pltpu.SemaphoreType.DMA((4, 2)),
        ],
        compiler_params=params(),
        name="slots",
    )(trainer, stays, arrived, *came, *passed)


def finish_kernel(scale, other, *refs):
    pieces, (out_hbm, rows, whole, parts, sems) = refs[:4], refs[-5:]
    me = lax.axis_index("brick")
    core, label = lax.rem(me, 2), label_of(me)
    half = 1 - core if other else core
    for k in range(4):
        at = pl.multiple_of(lax.bitwise_xor(label, k) * 48, 16)
        rows[pl.ds(at, 48), :] = pieces[k][...]
    size = 9 * C
    to = pl.multiple_of(2 * half * size, size)
    copies = [pltpu.make_async_copy(whole, out_hbm.at[pl.ds(to, size)], sems.at[9])]
    for i in range(8):
        block = rows[pl.ds(pl.multiple_of((i + 4 * half) * 16, 16), 16), :].astype(F32) * scale
        for tap in range(9):
            at = tap * C + i * 16
            whole[at : at + 16, :] = block[:, tap * C : (tap + 1) * C]
    copies[0].start()
    for i in range(4):
        at = pl.multiple_of((i + 8 - 8 * half) * 16, 16)
        block = rows[pl.ds(at, 16), :].astype(F32) * scale
        for tap in range(9):
            parts[tap, i * 16 : (i + 1) * 16, :] = block[:, tap * C : (tap + 1) * C]
    for tap in range(9):
        to = pl.multiple_of(size + tap * C + half * 64, 64)
        copies.append(
            pltpu.make_async_copy(parts.at[tap], out_hbm.at[pl.ds(to, 64)], sems.at[tap])
        )
        copies[-1].start()
    for copy in copies:
        copy.wait()


def finish_step(scale, pieces, before=None):
    other = before is not None
    return pl.pallas_call(
        functools.partial(finish_kernel, scale, other),
        in_specs=[VM] * 4 + [ANY] * other,
        out_specs=ANY,
        out_shape=shape((TAPS * C, C), F32),
        scratch_shapes=[
            pltpu.VMEM((192, 9 * C), BF16),
            pltpu.VMEM((9 * C, C), F32),
            pltpu.VMEM((9, 64, C), F32),
            pltpu.SemaphoreType.DMA((10,)),
        ],
        input_output_aliases={4: 0} if other else {},
        compiler_params=params(),
        name="finish_other" if other else "finish_own",
    )(*pieces, *([before] if other else []))


def label_of(me):
    z, y = lax.rem(lax.div(me, 2), 4), lax.div(me, 8)
    z, y = lax.bitwise_xor(z, lax.div(z, 2)), lax.bitwise_xor(y, lax.div(y, 2))
    return lax.rem(z, 2) + 2 * lax.rem(y, 2)


def swap(block, bits):
    pairs = [(i, i ^ bits) for i in range(lax.axis_size("brick"))]
    return lax.ppermute(block, "brick", pairs)


def shifted(block, distance):
    n = lax.axis_size("brick")
    return lax.ppermute(block, "brick", [(i, (i + distance) % n) for i in range(n)])


def shards(saved_inputs, saved_preacts, supervision, weights, trainer, counts):
    peers = lax.axis_size("brick")
    me = lax.axis_index("brick")
    layers = lax.axis_size("section")
    micros, own = saved_inputs.shape[1:3]
    slots = WORK * layers

    inputs = saved_inputs.reshape(WORK, VOX, C)
    preacts = saved_preacts.reshape(WORK, VOX, C)
    sup = supervision.reshape(WORK, VOX, C)
    above, came, pds = {}, [], []
    gin, deltas, gins, wn, preacts, sup, shares = first_step(counts, preacts, sup, weights[0])
    for slot in range(slots - 1):
        if slot > 0:
            arrived = [above[slot]] if slot >= WORK else []
            if slot == WORK + 2:
                shares, xt = lax.optimization_barrier([shares, transpose_step(inputs)])
            deltas, gins, gin, *pd = tick_step(
                slot, shares, preacts, sup, wn, deltas, gins, arrived
            )
            pds += pd
        sender = layers - 1 - slot // WORK
        if sender > 0:
            above[slot + WORK] = lax.ppermute(gin, "section", [(sender, sender - 1)])
        else:
            came.append(shifted(gin, 2))
    last = slots - 1
    *halves, pd = late_step(last, shares, preacts, sup, above[last], deltas, xt, pds)
    keep, send = halves[:4], halves[4:]
    send, came[0] = lax.optimization_barrier([send, came[0]])
    from_core = [swap(block, 1) for block in send]
    gin = last_step(last, gins, pd, wn)
    stays, leaves = select_step(trainer, gins, gin)
    from_core, came[1] = lax.optimization_barrier([from_core, came[1]])
    across = [(i, (i + 1 + 2 * (i % 2)) % peers) for i in range(peers)]
    arrived = lax.ppermute(leaves, "brick", across)

    part = [mine.astype(F32) + theirs.astype(F32) for mine, theirs in zip(keep, from_core)]
    total = part[0]
    for k in (2, 3, 1):
        block, bits = part[k], NEAR[k - 1]
        total = total + swap(block.astype(BF16), bits).astype(F32)
    total = total.astype(BF16)
    passed = [swap(block, 1) for block in came]
    total, passed = lax.optimization_barrier([total, passed])
    full = total.astype(F32)
    for bits in (24, 30, 6):
        full = full + swap(total, bits).astype(F32)
    full = full.astype(BF16)
    late = {bits: swap(full, bits) for bits in (8, 2, 10)}
    got = [late[bits] for bits in NEAR]
    came.append(shifted(gin, 2))
    passed.append(swap(came[3], 1))
    skip_grads = slots_step(trainer, stays, arrived, came, passed)
    got, skip_grads = lax.optimization_barrier([got, skip_grads])
    skip_grads = skip_grads.reshape((1, micros, 4) + saved_inputs.shape[3:])
    mine = [full] + got
    other = [swap(block, 1) for block in mine]
    scale = 1.0 / math.sqrt(WORK * peers * VOX)
    weight_grads = finish_step(scale, other, finish_step(scale, mine))
    return skip_grads, weight_grads[None]


def solution(mesh):
    bricks = P("section", None, "brick", None, None, None, None)
    in_specs = (bricks, bricks, bricks, P("section", None, None), P(), P(None, "brick"))
    out_specs = (bricks, P("section", None, None))
    return jax.shard_map(shards, mesh=mesh, in_specs=in_specs, out_specs=out_specs, check_vma=False)
```
